128 devices in a mesh: row: 4 (over y), col: 32 (over z, x, core).
Axes of the slice: x: 4, y: 4, z: 4, core: 2. Of those that a mesh axis runs over, the one named last changes fastest.
Arguments:
- top_boundary: bfloat16 [32, 8, 64, 1024], P('col'), may hold values from -6 to 6
- row_transfer: bfloat16 [4, 32, 8, 256, 256], P('row', 'col'), may hold values from -0.375 to 0.375
- proj_in: bfloat16 [4, 32, 8, 64, 1024], P('row', 'col'), may hold values from -3 to 3
- proj_out: bfloat16 [4, 32, 8, 64, 1024], P('row', 'col'), may hold values from -3 to 3
- bottom_boundary: bfloat16 [4, 32, 8, 64, 1024], P('row', 'col'), may hold values from -6 to 6
- environments: bfloat16 [4, 32, 8, 64, 64], P('row', 'col'), may hold values from -0.09375 to 0.09375
- operators: bfloat16 [2, 8, 16, 16], replicated, may hold values from -1.5 to 1.5
- ranks: int32 [4, 8], P('row'), may hold values from 32 to 64, as said below
Outputs:
- boundaries: bfloat16 [4, 32, 8, 64, 1024], P('row', 'col')
- log_norms: float32 [4, 8], P('row')
- observables: float32 [2, 4, 32, 8], P(None, 'row', 'col')
The draws below stay inside these ranges and needn't reach their ends.
Inputs may be any that keep to these rules, and one draw needn't show every extreme that they name: `ranks`: in every row at least one sector keeps all 64 slots.
All inputs are finite; a program needn't handle non-finite values.
Results may differ from the reference program's by a relative error of at most 0.034.
Values may be sent and summed in bfloat16 or wider, within the bound.
No kernel may reach another device: no remote copies, remote signals or barrier semaphores. Data moves between devices by JAX's collectives and lax.ppermute only.
A program may use at most 256 MiB of HBM per device.

```python
import math
import jax
import jax.numpy as jnp
from jax import lax

SEC = 8
PAD = 64
KM = 16
DB = 16
NCOL = 32
NROW = 4


def draw_ranks(key, part):
    key = jax.random.fold_in(key, 7)
    first_key, second_key = jax.random.split(key)
    base = jax.random.randint(first_key, (NROW, SEC), PAD // 2, PAD + 1)
    chosen = jax.random.randint(second_key, (NROW, 1), 0, SEC)
    sectors = jnp.arange(SEC, dtype=jnp.int32)[None, :]
    return jnp.where(sectors == chosen, PAD, base).astype(jnp.int32)


def graded_profile(key, span):
    phase_key, jitter_key = jax.random.split(key)
    phase = jax.random.uniform(phase_key, (), jnp.float32, 0.0, 2.0 * math.pi)
    columns = jnp.arange(NCOL, dtype=jnp.float32)
    wave = 0.5 + 0.5 * jnp.cos(2.0 * math.pi * columns / NCOL + phase)
    jitter = jax.random.uniform(jitter_key, (NROW, NCOL), jnp.float32, -0.05, 0.05)
    steep = (0.15 + span * wave)[None, :] + jitter
    steep = steep[:, :, None, None, None]
    outer = jnp.arange(PAD, dtype=jnp.float32) / (PAD - 1)
    inner = (jnp.arange(PAD * DB, dtype=jnp.int32) // DB).astype(jnp.float32) / (PAD - 1)
    exponent = steep * (outer[:, None] + inner[None, :])
    mean_square = jnp.expm1(2.0 * steep) / (2.0 * steep)
    return jnp.exp(exponent) / mean_square / math.sqrt(PAD * DB)


def draw_proj_in(key, part):
    key = jax.random.fold_in(key, 11)
    profile_key, noise_key = jax.random.split(key)
    shape = (NROW, NCOL, SEC, PAD, PAD * DB)
    noise = jax.random.truncated_normal(noise_key, -4.0, 4.0, shape, jnp.float32)
    span = 1.5
    return (noise * graded_profile(profile_key, span)).astype(jnp.bfloat16)


def draw_proj_out(key, part):
    key = jax.random.fold_in(key, 13)
    profile_key, noise_key = jax.random.split(key)
    shape = (NROW, NCOL, SEC, PAD, PAD * DB)
    noise = jax.random.truncated_normal(noise_key, -4.0, 4.0, shape, jnp.float32)
    span = 1.5
    return (noise * graded_profile(profile_key, span)).astype(jnp.bfloat16)


def block_levels(own_key, shape, shards, smallest, top_value):
    def one(position, blocks):
        steps = jax.random.uniform(jax.random.fold_in(jax.random.fold_in(own_key, 6), position), (blocks,), jnp.float32, smallest / len(shards), top_value / len(shards))
        return jnp.repeat(jnp.exp(steps), shape[position] // blocks).reshape((-1,) + (1,) * (len(shape) - position - 1))

    gain = one(*shards[0])
    for cut in shards[1:]:
        gain = gain * one(*cut)
    return gain


def centred(rng, shape, deviation, bound, cuts=(), kind=jnp.bfloat16):
    array = deviation * jax.random.normal(rng, shape, jnp.float32)
    if cuts:
        array = array * block_levels(rng, shape, cuts, -0.22, 0.18)
    return jnp.clip(array, -bound, bound).astype(kind)


def setup_inputs(seed: int = 0) -> dict:
    streams_of = jax.random.split(jax.random.key(seed), 9)
    top_boundary = centred(streams_of[0], (NCOL, SEC, PAD, KM * PAD), 1.0, 6.0, ((0, 32),))
    row_transfer = centred(streams_of[1], (NROW, NCOL, SEC, DB * KM, KM * DB), (DB * KM) ** -0.5, 0.375, ((0, 4), (1, 32)))
    proj_in = draw_proj_in(jax.random.fold_in(streams_of[8], 71), 0)
    proj_out = draw_proj_out(jax.random.fold_in(streams_of[8], 71), 0)
    bottom_boundary = centred(streams_of[4], (NROW, NCOL, SEC, PAD, KM * PAD), 1.0, 6.0, ((0, 4), (1, 32)))
    environments = centred(streams_of[5], (NROW, NCOL, SEC, PAD, PAD), (PAD * PAD) ** -0.5, 0.09375, ((0, 4), (1, 32)))
    operators = centred(streams_of[6], (2, SEC, KM, KM), KM ** -0.5, 1.5)
    ranks = draw_ranks(jax.random.fold_in(streams_of[8], 71), 0)
    return {"top_boundary": top_boundary, "row_transfer": row_transfer, "proj_in": proj_in, "proj_out": proj_out, "bottom_boundary": bottom_boundary, "environments": environments, "operators": operators, "ranks": ranks}


epsilon = 1e-06

def absorb_site(site, transfer, left_proj, right_proj, rank):
    upper = site.astype(jnp.float32).reshape(PAD, KM, PAD)
    left = left_proj.astype(jnp.float32).reshape(PAD, PAD, DB)
    first = jnp.einsum('caw,akb->cwkb', left, upper).astype(jnp.bfloat16)
    middle = transfer.astype(jnp.float32).reshape(DB, KM, KM, DB)
    second = jnp.einsum('cwkb,wkle->clbe', first.astype(jnp.float32), middle).astype(jnp.bfloat16)
    right = right_proj.astype(jnp.float32).reshape(PAD, PAD, DB)
    result = jnp.einsum('clbe,dbe->cld', second.astype(jnp.float32), right)
    inside = jnp.arange(PAD, dtype=jnp.int32) < rank
    keep = inside[:, None, None] & inside[None, None, :]
    return jnp.where(keep, result, jnp.zeros_like(result))

def observe_site(site, operators, left_env, right_env, lower):
    upper = site.astype(jnp.float32).reshape(PAD, KM, PAD)
    inserted = jnp.einsum('akb,qkl->qalb', upper, operators.astype(jnp.float32)).astype(jnp.bfloat16)
    carried = jnp.einsum('qalb,bd->qald', inserted.astype(jnp.float32), right_env.astype(jnp.float32)).astype(jnp.bfloat16)
    closed = jnp.einsum('qald,cld->qac', carried.astype(jnp.float32), lower.astype(jnp.float32).reshape(PAD, KM, PAD))
    return jnp.einsum('ac,qac->q', left_env.astype(jnp.float32), closed) / math.sqrt(KM)

def reference(top_boundary, row_transfer, proj_in, proj_out, bottom_boundary, environments, operators, ranks):
    current = top_boundary
    boundaries = []
    log_rows = []
    observed = []
    sector_absorb = jax.vmap(absorb_site, in_axes=(0, 0, 0, 0, 0))
    sector_observe = jax.vmap(observe_site, in_axes=(0, 1, 0, 0, 0))
    for row in range(NROW):
        following = jnp.roll(proj_out[row], -1, axis=0)
        rank_row = ranks[row]
        absorbed = lax.map(lambda pieces: sector_absorb(pieces[0], pieces[1], pieces[2], pieces[3], rank_row), (current, row_transfer[row], proj_in[row], following))
        norm = jnp.sqrt(lax.optimization_barrier(jnp.mean(absorbed * absorbed, axis=(0, 2, 3, 4))) + epsilon)
        current = (absorbed / norm[None, :, None, None, None]).astype(jnp.bfloat16).reshape(NCOL, SEC, PAD, KM * PAD)
        boundaries.append(current)
        log_rows.append(jnp.log(norm))
        right_envs = jnp.roll(environments[row], -1, axis=0)
        values = lax.map(lambda pieces: sector_observe(pieces[0], operators, pieces[1], pieces[2], pieces[3]), (current, environments[row], right_envs, bottom_boundary[row]))
        observed.append(values)
    observables = jnp.stack(observed).transpose(3, 0, 1, 2)
    return (jnp.stack(boundaries), jnp.stack(log_rows), observables)
```

```python
import math

import jax
import jax.numpy as jnp
from jax import lax
from jax.experimental import pallas as pl
from jax.experimental.pallas import tpu as pltpu
from jax.sharding import PartitionSpec as P

SEC = 8
PAD = 64
KM = 16
DB = 16
ROWS = 4
WIDE = 256
GROUPS = WIDE // PAD
SITE = KM * PAD

BF16 = jnp.bfloat16
F32 = jnp.float32

epsilon = 1e-06


def mm(a, b):
    return jnp.dot(a, b, preferred_element_type=F32)


def mmt(a, b):
    return lax.dot_general(a, b, (((1,), (1,)), ((), ())), preferred_element_type=F32)


def iota2(shape, dim):
    return lax.broadcasted_iota(jnp.int32, shape, dim)


def digit_swap():
    i, j = iota2((WIDE, WIDE), 0), iota2((WIDE, WIDE), 1)
    return jnp.where((i // 16 == j % 16) & (i % 16 == j // 16), 1.0, 0.0).astype(BF16)


def bond_swap():
    i, j = iota2((SITE, SITE), 0), iota2((SITE, SITE), 1)
    return ((i // DB == j % PAD) & (i % DB == j // PAD)).astype(BF16)


def total(x):
    return jnp.sum(jnp.sum(x, axis=1, keepdims=True), axis=0, keepdims=True)


def chain_kernel(
    pt_ref, q_ref, m_ref, perm_ref, u_ref, st_ref, bdm, bdq, xs, ys, pw, qw, stack
):
    swap = digit_swap()
    bdm[...] = jnp.zeros_like(bdm)
    bdq[...] = jnp.zeros_like(bdq)
    for src, dst in ((pt_ref.at[:, 0], pw), (q_ref.at[:, 0], qw)):
        acc = None
        for part in range(4):
            rows = src[:, part * PAD : (part + 1) * PAD, :].reshape(ROWS * PAD, WIDE)
            term = mm(rows, perm_ref[part * WIDE : (part + 1) * WIDE, :])
            acc = term if acc is None else acc + term
        dst[...] = acc.astype(BF16)
    for r in range(ROWS):
        site = m_ref if r == 0 else u_ref.at[r - 1]
        base = r * PAD
        for k in range(KM):
            lanes = slice(k * PAD, (k + 1) * PAD)
            block = site[:, lanes]
            right = qw[base : base + PAD, lanes]
            for g in range(GROUPS):
                at = slice(g * PAD, (g + 1) * PAD)
                bdm[k, at, at] = block
                bdq[at, k * WIDE + g * PAD : k * WIDE + (g + 1) * PAD] = right
                stack[k * 16 : (k + 1) * 16, at] = pw[base + g * 16 : base + (g + 1) * 16, lanes]
        left = mm(swap, stack[...]).astype(BF16)
        middle = mm(mmt(swap, pt_ref[r, 1]).astype(BF16), swap).astype(BF16)
        for k in range(KM):
            first = mm(left, bdm[k]).astype(BF16)
            xs[:, k * 16 : (k + 1) * 16, :] = first.reshape(16, 16, WIDE)
        for c in range(16):
            second = mm(middle, xs[c]).astype(BF16)
            for e in range(DB):
                ys[c * 16 : (c + 1) * 16, e * WIDE : (e + 1) * WIDE] = second[e * 16 : (e + 1) * 16]
        z = mmt(ys[...], bdq[...])
        top = jnp.max(jnp.max(jnp.abs(z), axis=1, keepdims=True), axis=0, keepdims=True)
        top = jnp.where(top > 0, top, 1.0)
        u = z / top
        st_ref[2 * r : 2 * r + 1, :] = jnp.broadcast_to(top, (1, 128))
        st_ref[2 * r + 1 : 2 * r + 2, :] = jnp.broadcast_to(total(u * u), (1, 128))
        placed = mm(swap, u.astype(BF16)).astype(BF16)
        for l in range(KM):
            for g in range(GROUPS):
                u_ref[r, g * 16 : (g + 1) * 16, l * PAD : (l + 1) * PAD] = placed[
                    l * 16 : (l + 1) * 16, g * PAD : (g + 1) * PAD
                ]


def vmem(count):
    return [pl.BlockSpec(memory_space=pltpu.VMEM)] * count


def chain(pt, q, m, perm, name):
    return pl.pallas_call(
        chain_kernel,
        out_shape=(
            jax.ShapeDtypeStruct((ROWS, PAD, SITE), BF16),
            jax.ShapeDtypeStruct((2 * ROWS, 128), F32),
        ),
        in_specs=vmem(4),
        out_specs=tuple(vmem(2)),
        scratch_shapes=[
            pltpu.VMEM((KM, WIDE, WIDE), BF16),
            pltpu.VMEM((WIDE, DB * WIDE), BF16),
            pltpu.VMEM((16, WIDE, WIDE), BF16),
            pltpu.VMEM((WIDE, DB * WIDE), BF16),
            pltpu.VMEM((ROWS * PAD, SITE), BF16),
            pltpu.VMEM((ROWS * PAD, SITE), BF16),
            pltpu.VMEM((WIDE, WIDE), BF16),
        ],
        compiler_params=pltpu.CompilerParams(vmem_limit_bytes=24 << 20),
        cost_estimate=pl.CostEstimate(
            flops=8_000_000_000, bytes_accessed=4 << 20, transcendentals=0
        ),
        name=name,
    )(pt, q, m, perm)


def weight_kernel(b_ref, el_ref, er_ref, op_ref, w_ref, bde, stack):
    bde[...] = jnp.zeros_like(bde)
    spread = jnp.where(iota2((WIDE, KM), 0) // 16 == iota2((WIDE, KM), 1), 1.0, 0.0).astype(BF16)
    same = iota2((WIDE, WIDE), 0) % 16 == iota2((WIDE, WIDE), 1) % 16

    def sector(s, carry):
        upper = mm(el_ref[s], b_ref[s]).astype(BF16)
        for g in range(GROUPS):
            at = slice(g * PAD, (g + 1) * PAD)
            bde[at, at] = er_ref[s]
        for g in range(4):
            both = mmt(upper[:, g * WIDE : (g + 1) * WIDE], bde[...]).astype(BF16)
            for i in range(4):
                l = g * 4 + i
                for h in range(GROUPS):
                    stack[l * 16 : (l + 1) * 16, h * PAD : (h + 1) * PAD] = both[
                        h * 16 : (h + 1) * 16, i * PAD : (i + 1) * PAD
                    ]
        for q in range(2):
            grown = mmt(mm(spread, op_ref[q, s]).astype(BF16), spread)
            grown = jnp.where(same, grown, 0.0).astype(BF16)
            out = mm(grown, stack[...]).astype(BF16)
            for k in range(KM):
                for h in range(GROUPS):
                    w_ref[q, s, h * 16 : (h + 1) * 16, k * PAD : (k + 1) * PAD] = out[
                        k * 16 : (k + 1) * 16, h * PAD : (h + 1) * PAD
                    ]
        return carry

    lax.fori_loop(0, SEC, sector, 0)


def observable_weights(lower, left_env, right_env, operators):
    return pl.pallas_call(
        weight_kernel,
        out_shape=jax.ShapeDtypeStruct((2, SEC, PAD, SITE), BF16),
        in_specs=vmem(4),
        out_specs=vmem(1)[0],
        scratch_shapes=[pltpu.VMEM((WIDE, WIDE), BF16), pltpu.VMEM((WIDE, WIDE), BF16)],
        compiler_params=pltpu.CompilerParams(vmem_limit_bytes=16 << 20),
        cost_estimate=pl.CostEstimate(
            flops=4_000_000_000, bytes_accessed=4 << 20, transcendentals=0
        ),
        name="observable_weights",
    )(lower, left_env, right_env, operators)


def observe_kernel(u1_ref, u2_ref, w_ref, o_ref):
    values = jnp.zeros((2, SEC), F32)
    at_q, at_s = iota2((2, SEC), 0), iota2((2, SEC), 1)
    for s in range(SEC):
        u = (u1_ref, u2_ref)[s % 2][s // 2].astype(F32)
        for q in range(2):
            here = total(u * w_ref[q, s].astype(F32))
            values = jnp.where((at_q == q) & (at_s == s), here, values)
    o_ref[...] = values


def observe(u1, u2, weights):
    return pl.pallas_call(
        observe_kernel,
        out_shape=jax.ShapeDtypeStruct((2, SEC), F32),
        in_specs=vmem(3),
        out_specs=vmem(1)[0],
        compiler_params=pltpu.CompilerParams(vmem_limit_bytes=16 << 20),
        cost_estimate=pl.CostEstimate(flops=2_000_000, bytes_accessed=3 << 20, transcendentals=0),
        name="observe",
    )(u1, u2, weights)


def finish_kernel(entries, where_ref, g_ref, raw_ref, u1_ref, u2_ref, out_ref, log_ref, obs_ref):
    row, col = where_ref[0], where_ref[1]
    columns = g_ref.shape[0]
    scale = jnp.ones((columns, SEC), F32)
    factor = jnp.zeros((columns, SEC), F32)
    logs = jnp.zeros((1, SEC), F32)
    for r in range(ROWS):
        size = scale * g_ref[:, r * SEC : (r + 1) * SEC]
        squares = size * size * g_ref[:, (ROWS + r) * SEC : (ROWS + r + 1) * SEC]
        norm = jnp.sqrt(jnp.sum(squares, axis=0, keepdims=True) / entries + epsilon)
        scale = size / norm
        factor = jnp.where(row == r, scale, factor)
        logs = jnp.where(row == r, jnp.log(norm), logs)
    factor = jnp.sum(
        jnp.where(iota2((columns, SEC), 0) == col, factor, 0.0), axis=0, keepdims=True
    )
    log_ref[...] = logs
    obs_ref[...] = raw_ref[...] * (factor / math.sqrt(KM))
    for s in range(SEC):
        u = (u1_ref, u2_ref)[s % 2][s // 2].astype(F32)
        out_ref[s] = (u * factor[:, s : s + 1]).astype(BF16)


def finish(entries, where, gathered, raw, u1, u2):
    return pl.pallas_call(
        lambda *refs: finish_kernel(entries, *refs),
        out_shape=(
            jax.ShapeDtypeStruct((SEC, PAD, SITE), BF16),
            jax.ShapeDtypeStruct((1, SEC), F32),
            jax.ShapeDtypeStruct((2, SEC), F32),
        ),
        in_specs=[pl.BlockSpec(memory_space=pltpu.SMEM)] + vmem(4),
        out_specs=tuple(vmem(3)),
        compiler_params=pltpu.CompilerParams(vmem_limit_bytes=16 << 20),
        cost_estimate=pl.CostEstimate(flops=2_000_000, bytes_accessed=2 << 20, transcendentals=0),
        name="finish",
    )(where, gathered, raw, u1, u2)


def passed_along(block, axis, distance):
    devices = range(lax.axis_size(axis))
    route = [((i - distance) % len(devices), i) for i in devices]
    return lax.ppermute(block, axis, route)


def across_rows(block):
    return lax.all_to_all(block, "row", 0, 0)


def parts(x, k):
    x = x.reshape(ROWS, 2, PAD, GROUPS, WIDE)[:, k]
    return x.transpose(0, 2, 1, 3).reshape(ROWS, 1, WIDE, WIDE)


def on_device(
    top_boundary, row_transfer, proj_in, proj_out, bottom_boundary, environments, operators, ranks
):
    row, col = lax.axis_index("row"), lax.axis_index("col")
    columns = lax.axis_size("col")
    inside = jnp.arange(PAD, dtype=jnp.int32)[None, :, None] < ranks[0][:, None, None]
    zero = jnp.zeros((), BF16)
    lefts = jnp.where(inside, proj_in[0, 0], zero)
    rights = jnp.where(inside, proj_out[0, 0], zero)
    transfers = row_transfer[0, 0].reshape(ROWS, 2, WIDE, WIDE)
    envs = environments[0, 0]
    perm = bond_swap()

    def lefts_and_transfers(k):
        return jnp.concatenate([parts(lefts, k), transfers[:, k : k + 1]], axis=1)

    pt1 = across_rows(lefts_and_transfers(0))
    next1 = passed_along(parts(rights, 0), "col", -1)
    next2 = passed_along(parts(rights, 1), "col", -1)
    next_envs = passed_along(envs, "col", -1)
    q1 = across_rows(next1)
    pt2 = across_rows(lefts_and_transfers(1))
    q2 = across_rows(next2)
    weights = observable_weights(bottom_boundary[0, 0], envs, next_envs, operators)
    mine = lax.dynamic_slice_in_dim(top_boundary[0], 2 * row, 2, axis=0)
    u1, st1 = chain(pt1, q1, mine[0], perm, "chain_first")
    got1 = across_rows(u1)
    u2, st2 = chain(pt2, q2, mine[1], perm, "chain_second")
    got2 = across_rows(u2)
    stats = jnp.stack([st1[:, 0], st2[:, 0]])
    stats = across_rows(jnp.broadcast_to(stats[None], (ROWS, 2, 2 * ROWS)))
    stats = stats.reshape(SEC, ROWS, 2).transpose(2, 1, 0).reshape(1, 2 * ROWS * SEC)
    gathered = lax.all_to_all(
        jnp.broadcast_to(stats[None], (columns, 1, 2 * ROWS * SEC)), "col", 0, 0
    ).reshape(columns, 2 * ROWS * SEC)
    raw = observe(got1, got2, weights)
    entries = float(columns * PAD * KM * PAD)
    place = jnp.stack([row, col]).astype(jnp.int32)
    sites, logs, values = finish(entries, place, gathered, raw, got1, got2)
    return sites[None, None], logs, values[:, None, None]


def solution(mesh):
    in_specs = (
        P("col", None, None, None),
        P("row", "col", None, None, None),
        P("row", "col", None, None, None),
        P("row", "col", None, None, None),
        P("row", "col", None, None, None),
        P("row", "col", None, None, None),
        P(),
        P("row", None),
    )
    out_specs = (P("row", "col", None, None, None), P("row", None), P(None, "row", "col", None))
    return jax.shard_map(
        on_device, mesh=mesh, in_specs=in_specs, out_specs=out_specs, check_vma=False
    )
```

```python
import math

import jax
import jax.numpy as jnp
from jax import lax
from jax.experimental import pallas as pl
from jax.experimental.pallas import tpu as pltpu
from jax.sharding import PartitionSpec as P

SEC = 8
PAD = 64
KM = 16
DB = 16
ROWS = 4
WIDE = 256
GROUPS = WIDE // PAD
SITE = KM * PAD
LANES = 128

BF16 = jnp.bfloat16
F32 = jnp.float32

epsilon = 1e-06


def mm(a, b):
    return jnp.dot(a, b, preferred_element_type=F32)


def mmt(a, b):
    return lax.dot_general(a, b, (((1,), (1,)), ((), ())), preferred_element_type=F32)


def iota2(shape, dim):
    return lax.broadcasted_iota(jnp.int32, shape, dim)


def digit_swap():
    i, j = iota2((WIDE, WIDE), 0), iota2((WIDE, WIDE), 1)
    return jnp.where((i // 16 == j % 16) & (i % 16 == j // 16), 1.0, 0.0).astype(BF16)


def bond_swap():
    i, j = iota2((SITE, SITE), 0), iota2((SITE, SITE), 1)
    return jnp.where(j == (i % DB) * PAD + i // DB, 1.0, 0.0).astype(BF16)


def total(x):
    return jnp.sum(jnp.sum(x, axis=1, keepdims=True), axis=0, keepdims=True)


def vmem(count):
    return [pl.BlockSpec(memory_space=pltpu.VMEM)] * count


def smem():
    return pl.BlockSpec(memory_space=pltpu.SMEM)


def masked(block, inside):
    return jnp.where(inside, block.astype(F32), 0.0).astype(BF16)


def pack_first_kernel(me_ref, rank_ref, p_ref, t_ref, q_ref, *refs):
    outs, rights, (held, sems) = refs[:ROWS], refs[ROWS : ROWS + 2], refs[ROWS + 2 :]
    me = me_ref[0]
    at = iota2((PAD, WIDE), 0)
    copies = []
    for x in range(ROWS):
        s = 2 * (me ^ x)
        copies.append(
            (
                pltpu.make_async_copy(p_ref.at[s], held.at[x], sems.at[0, x]),
                pltpu.make_async_copy(t_ref.at[s], outs[x].at[1], sems.at[1, x]),
                pltpu.make_async_copy(q_ref.at[s], rights[0].at[x], sems.at[2, x]),
                pltpu.make_async_copy(q_ref.at[s + 1], rights[1].at[x], sems.at[3, x]),
            )
        )
    for group in copies:
        for copy in group:
            copy.start()
    for x in range(ROWS):
        inside = at < rank_ref[0, 2 * (me ^ x)]
        copies[x][0].wait()
        for g in range(GROUPS):
            outs[x][0, g * PAD : (g + 1) * PAD, :] = masked(
                held[x, :, g * WIDE : (g + 1) * WIDE], inside
            )
    for group in copies:
        for copy in group[1:]:
            copy.wait()


def pack_first(me, ranks, p, t, q):
    piece = jax.ShapeDtypeStruct((2, WIDE, WIDE), BF16)
    right = jax.ShapeDtypeStruct((ROWS, PAD, SITE), BF16)
    return pl.pallas_call(
        pack_first_kernel,
        out_shape=(piece,) * ROWS + (right,) * 2,
        in_specs=[smem(), smem()] + [pl.BlockSpec(memory_space=pl.ANY)] * 3,
        out_specs=tuple(vmem(ROWS + 2)),
        scratch_shapes=[pltpu.VMEM((ROWS, PAD, SITE), BF16), pltpu.SemaphoreType.DMA((4, ROWS))],
        compiler_params=pltpu.CompilerParams(vmem_limit_bytes=56 << 20),
        cost_estimate=pl.CostEstimate(flops=1_000_000, bytes_accessed=2 << 20, transcendentals=0),
        name="pack_first",
    )(me, ranks, p, t, q)


def pack_second_kernel(me_ref, rank_ref, p_ref, t_ref, q1_ref, q2_ref, ready_ref, *refs):
    firsts, seconds = refs[:ROWS], refs[ROWS : 2 * ROWS]
    held, sems = refs[2 * ROWS :]
    me = me_ref[0]
    at = iota2((PAD, WIDE), 0)
    copies = []
    for x in range(ROWS):
        s = 2 * (me ^ x) + 1
        copies.append(
            (
                pltpu.make_async_copy(p_ref.at[s], held.at[x], sems.at[0, x]),
                pltpu.make_async_copy(t_ref.at[s], seconds[x].at[1], sems.at[1, x]),
            )
        )
    for pair in copies:
        for copy in pair:
            copy.start()
    for x in range(ROWS):
        s = 2 * (me ^ x)
        inside = [at < rank_ref[0, s + k] for k in range(2)]
        copies[x][0].wait()
        for g in range(GROUPS):
            rows, lanes = slice(g * PAD, (g + 1) * PAD), slice(g * WIDE, (g + 1) * WIDE)
            seconds[x][0, rows, :] = masked(held[x, :, lanes], inside[1])
            firsts[x][rows, :] = masked(q1_ref[x, :, lanes], inside[0])
            seconds[x][2, rows, :] = masked(q2_ref[x, :, lanes], inside[1])
    for x in range(ROWS):
        copies[x][1].wait()


def pack_second(me, ranks, p, t, q1, q2, ready):
    one = jax.ShapeDtypeStruct((WIDE, WIDE), BF16)
    three = jax.ShapeDtypeStruct((3, WIDE, WIDE), BF16)
    return pl.pallas_call(
        pack_second_kernel,
        out_shape=(one,) * ROWS + (three,) * ROWS,
        in_specs=[smem(), smem()] + [pl.BlockSpec(memory_space=pl.ANY)] * 2 + vmem(3),
        out_specs=tuple(vmem(2 * ROWS)),
        scratch_shapes=[pltpu.VMEM((ROWS, PAD, SITE), BF16), pltpu.SemaphoreType.DMA((2, ROWS))],
        compiler_params=pltpu.CompilerParams(vmem_limit_bytes=8 << 20),
        cost_estimate=pl.CostEstimate(flops=1_000_000, bytes_accessed=4 << 20, transcendentals=0),
        name="pack_second",
    )(me, ranks, p, t, q1, q2, ready)


def chain_kernel(
    me_ref, pts, qs, m_ref, perm_ref, before_ref, befores, us, st_ref,
    bdm, bdq, xs, ys, qw, pw, lefts, middles, stack, site, sem,
):
    me = me_ref[0]
    start = pltpu.make_async_copy(m_ref.at[2 * me + len(befores) // ROWS], site, sem)
    start.start()
    swap = digit_swap()
    bdm[...] = jnp.zeros_like(bdm)
    bdq[...] = jnp.zeros_like(bdq)
    for pieces, dst in (([ref.at[0] for ref in pts], pw), (qs, qw)):
        acc = None
        for part in range(GROUPS):
            rows = jnp.concatenate([ref[part * PAD : (part + 1) * PAD, :] for ref in pieces], axis=0)
            term = mm(rows, perm_ref[part * WIDE : (part + 1) * WIDE, :])
            acc = term if acc is None else acc + term
        dst[...] = acc.astype(BF16)
    for x in range(ROWS):
        for w in range(DB):
            for g in range(GROUPS):
                stack[w * 16 : (w + 1) * 16, g * PAD : (g + 1) * PAD] = pw[
                    x * PAD + g * 16 : x * PAD + (g + 1) * 16, w * PAD : (w + 1) * PAD
                ]
        lefts[me ^ x] = mm(swap, stack[...]).astype(BF16)
        middles[me ^ x] = mm(mmt(swap, pts[x][1]).astype(BF16), swap).astype(BF16)
    start.wait()
    for x in range(len(befores)):
        us[x][0] = befores[x][0]

    def row(r, carry):
        base = pl.multiple_of((me ^ r) * PAD, PAD)
        for k in range(KM):
            lanes = slice(k * PAD, (k + 1) * PAD)
            block = site[:, lanes]
            right = qw[pl.ds(base, PAD), lanes]
            for g in range(GROUPS):
                at = slice(g * PAD, (g + 1) * PAD)
                bdm[k, at, at] = block
                bdq[at, k * WIDE + g * PAD : k * WIDE + (g + 1) * PAD] = right
        left = lefts[r]
        middle = middles[r]
        for k in range(KM):
            first = mm(left, bdm[k]).astype(BF16)
            xs[:, k * 16 : (k + 1) * 16, :] = first.reshape(16, 16, WIDE)
        for c in range(16):
            second = mm(middle, xs[c]).astype(BF16)
            for e in range(DB):
                ys[c * 16 : (c + 1) * 16, e * WIDE : (e + 1) * WIDE] = second[e * 16 : (e + 1) * 16]
        z = mmt(ys[...], bdq[...])
        top = jnp.max(jnp.max(jnp.abs(z), axis=1, keepdims=True), axis=0, keepdims=True)
        top = jnp.where(top > 0, top, 1.0)
        u = z / top
        placed = mm(swap, u.astype(BF16)).astype(BF16)
        for l in range(KM):
            for g in range(GROUPS):
                site[g * 16 : (g + 1) * 16, l * PAD : (l + 1) * PAD] = placed[
                    l * 16 : (l + 1) * 16, g * PAD : (g + 1) * PAD
                ]
        for x in range(ROWS):

            @pl.when(r == me ^ x)
            def _(x=x):
                us[x][len(befores) // ROWS] = site[...]

        lane = iota2((1, LANES), 1)
        carry = jnp.where(lane == 2 * r, top, carry)
        return jnp.where(lane == 2 * r + 1, total(u * u), carry)

    stats = lax.fori_loop(0, ROWS, row, jnp.zeros((1, LANES), F32))
    if befores:
        lane = iota2((1, LANES), 1)
        stats = jnp.where(lane < 2 * ROWS, before_ref[0:1, :], pltpu.roll(stats, 2 * ROWS, 1))
    st_ref[...] = jnp.broadcast_to(stats, st_ref.shape)


def chain(me, pts, qs, m, perm, before, befores, copies, name):
    inputs = [me, *pts, *(qs or ()), perm, *([before] if befores else []), *befores, m]
    sites = 2 if befores else 1

    def body(*refs):
        me_ref, *refs = refs
        pt_refs, refs = refs[:ROWS], refs[ROWS:]
        if qs is None:
            q_refs = [ref.at[2] for ref in pt_refs]
        else:
            q_refs, refs = refs[:ROWS], refs[ROWS:]
        perm_ref, *refs = refs
        before_ref = None
        if befores:
            before_ref, *refs = refs
        before_sites, refs = refs[: len(befores)], refs[len(befores) :]
        m_ref, *refs = refs
        us, (st_ref, *scratch) = refs[:ROWS], refs[ROWS:]
        chain_kernel(
            me_ref, pt_refs, q_refs, m_ref, perm_ref, before_ref, before_sites, us, st_ref, *scratch
        )

    site = jax.ShapeDtypeStruct((sites, PAD, SITE), BF16)
    return pl.pallas_call(
        body,
        out_shape=(site,) * ROWS + (jax.ShapeDtypeStruct((copies, LANES), F32),),
        in_specs=[smem()] + vmem(len(inputs) - 2) + [pl.BlockSpec(memory_space=pl.ANY)],
        out_specs=tuple(vmem(ROWS + 1)),
        scratch_shapes=[
            pltpu.VMEM((KM, WIDE, WIDE), BF16),
            pltpu.VMEM((WIDE, DB * WIDE), BF16),
            pltpu.VMEM((16, WIDE, WIDE), BF16),
            pltpu.VMEM((WIDE, DB * WIDE), BF16),
            pltpu.VMEM((ROWS * PAD, SITE), BF16),
            pltpu.VMEM((ROWS * PAD, SITE), BF16),
            pltpu.VMEM((ROWS, WIDE, WIDE), BF16),
            pltpu.VMEM((ROWS, WIDE, WIDE), BF16),
            pltpu.VMEM((WIDE, WIDE), BF16),
            pltpu.VMEM((PAD, SITE), BF16),
            pltpu.SemaphoreType.DMA,
        ],
        compiler_params=pltpu.CompilerParams(vmem_limit_bytes=24 << 20),
        cost_estimate=pl.CostEstimate(
            flops=12_000_000_000, bytes_accessed=4 << 20, transcendentals=0
        ),
        name=name,
    )(*inputs)


def weight_kernel(el_ref, er_ref, op_ref, lower_ref, w_ref, done_ref, perm_ref, bde, stack, b_ref, sem):
    copy = pltpu.make_async_copy(lower_ref, b_ref, sem)
    copy.start()
    done_ref[...] = jnp.zeros_like(done_ref)
    bde[...] = jnp.zeros_like(bde)
    spread = jnp.where(iota2((WIDE, KM), 0) // 16 == iota2((WIDE, KM), 1), 1.0, 0.0).astype(BF16)
    same = iota2((WIDE, WIDE), 0) % 16 == iota2((WIDE, WIDE), 1) % 16
    perm_ref[...] = bond_swap()
    copy.wait()

    def sector(s, carry):
        upper = mm(el_ref[s], b_ref[s]).astype(BF16)
        for g in range(GROUPS):
            at = slice(g * PAD, (g + 1) * PAD)
            bde[at, at] = er_ref[s]
        for g in range(4):
            both = mmt(upper[:, g * WIDE : (g + 1) * WIDE], bde[...]).astype(BF16)
            for i in range(4):
                l = g * 4 + i
                for h in range(GROUPS):
                    stack[l * 16 : (l + 1) * 16, h * PAD : (h + 1) * PAD] = both[
                        h * 16 : (h + 1) * 16, i * PAD : (i + 1) * PAD
                    ]
        for q in range(2):
            grown = mmt(mm(spread, op_ref[q, s]).astype(BF16), spread)
            grown = jnp.where(same, grown, 0.0).astype(BF16)
            out = mm(grown, stack[...]).astype(BF16)
            for k in range(KM):
                for h in range(GROUPS):
                    w_ref[q, s, h * 16 : (h + 1) * 16, k * PAD : (k + 1) * PAD] = out[
                        k * 16 : (k + 1) * 16, h * PAD : (h + 1) * PAD
                    ]
        return carry

    lax.fori_loop(0, SEC, sector, 0)


def observable_weights(lower, left_env, right_env, operators):
    return pl.pallas_call(
        weight_kernel,
        out_shape=(
            jax.ShapeDtypeStruct((2, SEC, PAD, SITE), BF16),
            jax.ShapeDtypeStruct((8, LANES), F32),
            jax.ShapeDtypeStruct((SITE, SITE), BF16),
        ),
        in_specs=vmem(3) + [pl.BlockSpec(memory_space=pl.ANY)],
        out_specs=tuple(vmem(3)),
        scratch_shapes=[
            pltpu.VMEM((WIDE, WIDE), BF16),
            pltpu.VMEM((WIDE, WIDE), BF16),
            pltpu.VMEM((SEC, PAD, SITE), BF16),
            pltpu.SemaphoreType.DMA,
        ],
        compiler_params=pltpu.CompilerParams(vmem_limit_bytes=16 << 20),
        cost_estimate=pl.CostEstimate(
            flops=6_000_000_000, bytes_accessed=4 << 20, transcendentals=0
        ),
        name="observable_weights",
    )(left_env, right_env, operators, lower)


def finish_kernel(entries, me_ref, g_ref, w_ref, *refs):
    us, (out_ref, log_ref, obs_ref) = refs[:ROWS], refs[ROWS:]
    row, col = me_ref[0], me_ref[1]
    columns = g_ref.shape[0] // ROWS
    at_s = iota2((1, SEC), 1)
    at_qs, at_q = iota2((2, SEC), 1), iota2((2, SEC), 0)
    logs = jnp.zeros((1, SEC), F32)
    factors = []
    for i in range(ROWS):
        for k in range(2):
            scale = jnp.ones((columns, 1), F32)
            factor = jnp.zeros((columns, 1), F32)
            log = jnp.zeros((1, 1), F32)
            here = pl.ds(i * columns, columns)
            for r in range(ROWS):
                lane = 2 * ROWS * k + 2 * r
                size = scale * g_ref[here, lane : lane + 1]
                squares = size * size * g_ref[here, lane + 1 : lane + 2]
                norm = jnp.sqrt(jnp.sum(squares, axis=0, keepdims=True) / entries + epsilon)
                scale = size / norm
                factor = jnp.where(row == r, scale, factor)
                log = jnp.where(row == r, jnp.log(norm), log)
            at_col = iota2((columns, 1), 0) == col
            factors.append(jnp.sum(jnp.where(at_col, factor, 0.0), axis=0, keepdims=True))
            logs = jnp.where(at_s == 2 * i + k, log, logs)
    log_ref[...] = logs
    values = jnp.zeros((2, SEC), F32)
    for k in range(2):
        for x in range(ROWS):
            i = row ^ x
            s = 2 * i + k
            factor = factors[k]
            for other in range(1, ROWS):
                factor = jnp.where(i == other, factors[2 * other + k], factor)
            u = us[x][k].astype(F32) * factor
            out_ref[s] = u.astype(BF16)
            for q in range(2):
                value = total(u * w_ref[q, s].astype(F32))
                values = jnp.where((at_q == q) & (at_qs == s), value, values)
    obs_ref[...] = values / math.sqrt(KM)


def finish(entries, me, gathered, weights, us):
    return pl.pallas_call(
        lambda *refs: finish_kernel(entries, *refs),
        out_shape=(
            jax.ShapeDtypeStruct((SEC, PAD, SITE), BF16),
            jax.ShapeDtypeStruct((1, SEC), F32),
            jax.ShapeDtypeStruct((2, SEC), F32),
        ),
        in_specs=[smem()] + vmem(2 + len(us)),
        out_specs=tuple(vmem(3)),
        compiler_params=pltpu.CompilerParams(vmem_limit_bytes=16 << 20),
        cost_estimate=pl.CostEstimate(flops=2_000_000, bytes_accessed=2 << 20, transcendentals=0),
        name="finish",
    )(me, gathered, weights, *us)


def passed_along(block, axis, distance):
    devices = range(lax.axis_size(axis))
    route = [((i - distance) % len(devices), i) for i in devices]
    return lax.ppermute(block, axis, route)


def exchanged(block, x):
    return lax.ppermute(block, "row", [(i, i ^ x) for i in range(ROWS)])


NEAR_FIRST = (1, 3, 2)


def exchanged_all(blocks):
    got = {x: exchanged(blocks[x], x) for x in NEAR_FIRST}
    return [blocks[0]] + [got[x] for x in range(1, ROWS)]


def on_device(
    top_boundary, row_transfer, proj_in, proj_out, bottom_boundary, environments, operators, ranks
):
    row, col = lax.axis_index("row"), lax.axis_index("col")
    columns = lax.axis_size("col")
    me = jnp.stack([row, col]).astype(jnp.int32)
    envs = environments[0, 0]
    lefts, transfers = proj_in[0, 0], row_transfer[0, 0]
    *pts1, q1, q2 = pack_first(me, ranks, lefts, transfers, proj_out[0, 0])
    q1 = passed_along(q1, "col", -1)
    q2 = passed_along(q2, "col", -1)
    next_envs = passed_along(envs, "col", -1)
    pts1 = exchanged_all(pts1)
    weights, ready, perm = observable_weights(bottom_boundary[0, 0], envs, next_envs, operators)
    packed = pack_second(me, ranks, lefts, transfers, q1, q2, ready)
    qs1 = exchanged_all(packed[:ROWS])
    ptqs2 = exchanged_all(packed[ROWS:])
    top = top_boundary[0]
    *us1, stats = chain(me, pts1, qs1, top, perm, None, (), 8, "chain_first")
    everyone = ROWS * columns
    *us, stats = chain(me, ptqs2, None, top, perm, stats, us1, everyone, "chain_second")
    us = exchanged_all(us)
    gathered = lax.all_to_all(stats, ("row", "col"), 0, 0, tiled=True)
    entries = float(columns * PAD * KM * PAD)
    sites, logs, values = finish(entries, me, gathered, weights, us)
    return sites[None, None], logs, values[:, None, None]


def solution(mesh):
    in_specs = (
        P("col", None, None, None),
        P("row", "col", None, None, None),
        P("row", "col", None, None, None),
        P("row", "col", None, None, None),
        P("row", "col", None, None, None),
        P("row", "col", None, None, None),
        P(),
        P("row", None),
    )
    out_specs = (P("row", "col", None, None, None), P("row", None), P(None, "row", "col", None))
    return jax.shard_map(
        on_device, mesh=mesh, in_specs=in_specs, out_specs=out_specs, check_vma=False
    )
```

```python
import math

import jax
import jax.numpy as jnp
import numpy as np
from jax import lax
from jax.experimental import pallas as pl
from jax.experimental.pallas import tpu as pltpu
from jax.sharding import PartitionSpec as P

SEC = 8
PAD = 64
KM = 16
DB = 16
ROWS = 4
WIDE = 256
GROUPS = WIDE // PAD
SITE = KM * PAD
LANES = 128

BF16 = jnp.bfloat16
F32 = jnp.float32

epsilon = 1e-06


def mm(a, b):
    return jnp.dot(a, b, preferred_element_type=F32)


def mmt(a, b):
    return lax.dot_general(a, b, (((1,), (1,)), ((), ())), preferred_element_type=F32)


def iota2(shape, dim):
    return lax.broadcasted_iota(jnp.int32, shape, dim)


def digit_swap():
    i, j = iota2((WIDE, WIDE), 0), iota2((WIDE, WIDE), 1)
    return jnp.where((i // 16 == j % 16) & (i % 16 == j // 16), 1.0, 0.0).astype(BF16)


def bond_swap():
    i = np.arange(SITE)
    matrix = np.zeros((SITE, SITE), np.float32)
    matrix[i, (i % DB) * PAD + i // DB] = 1.0
    return jnp.asarray(matrix, BF16)


def total(x):
    return jnp.sum(jnp.sum(x, axis=1, keepdims=True), axis=0, keepdims=True)


def vmem(count):
    return [pl.BlockSpec(memory_space=pltpu.VMEM)] * count


def smem():
    return pl.BlockSpec(memory_space=pltpu.SMEM)


def masked(block, inside):
    return jnp.where(inside, block.astype(F32), 0.0).astype(BF16)


def anywhere(count):
    return [pl.BlockSpec(memory_space=pl.ANY)] * count


def params(mib):
    return pltpu.CompilerParams(vmem_limit_bytes=mib << 20)


def light(mib):
    return pl.CostEstimate(flops=1_000_000, bytes_accessed=mib << 20, transcendentals=0)


def pack_kernel(k, rank_ref, p_ref, t_ref, after_ref, *refs):
    rights, raws = (), ()
    if k == 0:
        q_ref, *refs = refs
        outs, raws, (held, sems) = refs[:ROWS], refs[ROWS : ROWS + 2], refs[ROWS + 2 :]
    else:
        *rights, outs, held, sems = refs[0], refs[1 : ROWS + 1], refs[ROWS + 1], refs[ROWS + 2]
    me = lax.axis_index("row")
    at = iota2((PAD, WIDE), 0)
    copies = []
    for x in range(ROWS):
        s = 2 * (me ^ x) + k
        copies.append(
            (
                pltpu.make_async_copy(p_ref.at[s], held.at[x], sems.at[0, x]),
                pltpu.make_async_copy(t_ref.at[s], outs[x].at[1], sems.at[1, x]),
            )
        )
    picks = [
        pltpu.make_async_copy(q_ref.at[2 * (me ^ x) + j], raws[j].at[x], sems.at[2 + j, x])
        for j in range(len(raws))
        for x in range(ROWS)
    ]
    for pair in copies:
        for copy in pair:
            copy.start()
    for copy in picks:
        copy.start()
    for x in range(ROWS):
        inside = at < rank_ref[0, 2 * (me ^ x) + k]
        copies[x][0].wait()
        for g in range(GROUPS):
            rows, lanes = slice(g * PAD, (g + 1) * PAD), slice(g * WIDE, (g + 1) * WIDE)
            outs[x][0, rows, :] = masked(held[x, :, lanes], inside)
            if k == 1:
                outs[x][2, rows, :] = masked(rights[0][x, :, lanes], inside)
    for x in range(ROWS):
        copies[x][1].wait()
    for copy in picks:
        copy.wait()


def pack(k, ranks, p, t, after, *rights):
    raws = () if k else (jax.ShapeDtypeStruct((ROWS, PAD, SITE), BF16),) * 2
    return pl.pallas_call(
        lambda *refs: pack_kernel(k, *refs),
        out_shape=(jax.ShapeDtypeStruct((2 + k, WIDE, WIDE), BF16),) * ROWS + raws,
        in_specs=[smem()] + anywhere(3) + (vmem(1) if k else anywhere(1)),
        out_specs=tuple(vmem(ROWS + len(raws))),
        scratch_shapes=[pltpu.VMEM((ROWS, PAD, SITE), BF16), pltpu.SemaphoreType.DMA((4, ROWS))],
        compiler_params=params(8 if k else 56),
        cost_estimate=light(2),
        name="pack_second" if k else "pack_first",
    )(ranks, p, t, after, *rights)


def mask_rights_kernel(rank_ref, after_ref, q_ref, *outs):
    me = lax.axis_index("row")
    at = iota2((PAD, WIDE), 0)
    for x in range(ROWS):
        inside = at < rank_ref[0, 2 * (me ^ x)]
        for g in range(GROUPS):
            rows, lanes = slice(g * PAD, (g + 1) * PAD), slice(g * WIDE, (g + 1) * WIDE)
            outs[x][rows, :] = masked(q_ref[x, :, lanes], inside)


def mask_rights(ranks, after, q):
    return pl.pallas_call(
        mask_rights_kernel,
        out_shape=(jax.ShapeDtypeStruct((WIDE, WIDE), BF16),) * ROWS,
        in_specs=[smem()] + anywhere(1) + vmem(1),
        out_specs=tuple(vmem(ROWS)),
        compiler_params=params(8),
        cost_estimate=light(1),
        name="mask_rights",
    )(ranks, after, q)


def chain_kernel(
    pts, qs, m_ref, perm_ref, before_ref, befores, us, st_ref,
    bdm, bdq, xs, ys, qw, pw, lefts, middles, stack, site, place, zs, held, sem,
):
    me = lax.axis_index("row")
    k0 = len(befores) // ROWS
    start = pltpu.make_async_copy(m_ref.at[2 * me + k0], site, sem)
    start.start()
    swap = digit_swap()
    bdm[...] = jnp.zeros_like(bdm)
    bdq[...] = jnp.zeros_like(bdq)
    for pieces, dst in (([ref.at[0] for ref in pts], pw), (qs, qw)):
        acc = None
        for part in range(GROUPS):
            rows = jnp.concatenate([ref[part * PAD : (part + 1) * PAD, :] for ref in pieces], axis=0)
            term = mm(rows, perm_ref[part * WIDE : (part + 1) * WIDE, :])
            acc = term if acc is None else acc + term
        dst[...] = acc.astype(BF16)
    for x in range(ROWS):
        for w in range(DB):
            for g in range(GROUPS):
                stack[x, w * 16 : (w + 1) * 16, g * PAD : (g + 1) * PAD] = pw[
                    x * PAD + g * 16 : x * PAD + (g + 1) * 16, w * PAD : (w + 1) * PAD
                ]
    for x in range(ROWS):
        lefts[me ^ x] = mm(swap, stack[x]).astype(BF16)
        middles[me ^ x] = mm(mmt(swap, pts[x][1]).astype(BF16), swap).astype(BF16)
    start.wait()
    for x in range(len(befores)):
        us[x][0] = befores[x][0]
    lane = iota2((1, LANES), 1)
    stats = jnp.zeros((1, LANES), F32)
    inverse = None
    for r in range(ROWS):
        base = pl.multiple_of((me ^ r) * PAD, PAD)
        left, middle = lefts[r], middles[r]
        for k in range(KM):
            lanes = slice(k * PAD, (k + 1) * PAD)
            right = qw[pl.ds(base, PAD), lanes]
            for g in range(GROUPS):
                at = slice(g * PAD, (g + 1) * PAD)
                if r == 0:
                    bdm[k, at, at] = site[:, lanes]
                else:
                    for h in range(GROUPS):
                        bdm[k, g * PAD + h * 16 : g * PAD + (h + 1) * 16, at] = place[
                            k * 16 : (k + 1) * 16, h * PAD : (h + 1) * PAD
                        ]
                bdq[r % 2, at, k * WIDE + g * PAD : k * WIDE + (g + 1) * PAD] = right
            first = mm(left, bdm[k]).astype(BF16)
            xs[:, k * 16 : (k + 1) * 16, :] = first.reshape(16, 16, WIDE)
        for c in range(16):
            second = mm(middle, xs[c]).astype(BF16)
            for e in range(DB):
                ys[c * 16 : (c + 1) * 16, e * WIDE : (e + 1) * WIDE] = second[e * 16 : (e + 1) * 16]
            if r > 0:
                for g in range(GROUPS):
                    held[r - 1, g * 16 : (g + 1) * 16, c * PAD : (c + 1) * PAD] = place[
                        c * 16 : (c + 1) * 16, g * PAD : (g + 1) * PAD
                    ]

        @pl.when(me >= 0)
        def _(r=r):
            zs[...] = mmt(ys[...], bdq[r % 2])

        z = zs[...]
        if inverse is not None:
            z = z * inverse
        place[...] = mm(swap, z.astype(BF16)).astype(BF16)
        top = jnp.max(jnp.max(jnp.abs(z), axis=1, keepdims=True), axis=0, keepdims=True)
        top = jnp.where(top > 0, top, 1.0)
        inverse = 1.0 / top
        stats = jnp.where(lane == 2 * r, top, stats)
        stats = jnp.where(lane == 2 * r + 1, total(z * z), stats)
    for c in range(KM):
        for g in range(GROUPS):
            held[ROWS - 1, g * 16 : (g + 1) * 16, c * PAD : (c + 1) * PAD] = place[
                c * 16 : (c + 1) * 16, g * PAD : (g + 1) * PAD
            ]
    for x in range(ROWS):
        us[x][k0] = held[me ^ x]
    if befores:
        stats = jnp.where(lane < 2 * ROWS, before_ref[0:1, :], pltpu.roll(stats, 2 * ROWS, 1))
    st_ref[...] = jnp.broadcast_to(stats, st_ref.shape)


def chain(pts, qs, m, perm, before, befores, after, copies, name):
    inputs = [*pts, *(qs or ()), perm, *([before] if befores else []), *befores, after, m]
    sites = 2 if befores else 1

    def body(*refs):
        pt_refs, refs = refs[:ROWS], refs[ROWS:]
        if qs is None:
            q_refs = [ref.at[2] for ref in pt_refs]
        else:
            q_refs, refs = refs[:ROWS], refs[ROWS:]
        perm_ref, *refs = refs
        before_ref = None
        if befores:
            before_ref, *refs = refs
        before_sites, refs = refs[: len(befores)], refs[len(befores) :]
        _, m_ref, *refs = refs
        us, (st_ref, *scratch) = refs[:ROWS], refs[ROWS:]
        chain_kernel(
            pt_refs, q_refs, m_ref, perm_ref, before_ref, before_sites, us, st_ref, *scratch
        )

    site = jax.ShapeDtypeStruct((sites, PAD, SITE), BF16)
    return pl.pallas_call(
        body,
        out_shape=(site,) * ROWS + (jax.ShapeDtypeStruct((copies, LANES), F32),),
        in_specs=vmem(len(inputs) - 2) + anywhere(2),
        out_specs=tuple(vmem(ROWS + 1)),
        scratch_shapes=[
            pltpu.VMEM((KM, WIDE, WIDE), BF16),
            pltpu.VMEM((2, WIDE, DB * WIDE), BF16),
            pltpu.VMEM((16, WIDE, WIDE), BF16),
            pltpu.VMEM((WIDE, DB * WIDE), BF16),
            pltpu.VMEM((ROWS * PAD, SITE), BF16),
            pltpu.VMEM((ROWS * PAD, SITE), BF16),
            pltpu.VMEM((ROWS, WIDE, WIDE), BF16),
            pltpu.VMEM((ROWS, WIDE, WIDE), BF16),
            pltpu.VMEM((ROWS, WIDE, WIDE), BF16),
            pltpu.VMEM((PAD, SITE), BF16),
            pltpu.VMEM((WIDE, WIDE), BF16),
            pltpu.VMEM((WIDE, WIDE), F32),
            pltpu.VMEM((ROWS, PAD, SITE), BF16),
            pltpu.SemaphoreType.DMA,
        ],
        compiler_params=pltpu.CompilerParams(vmem_limit_bytes=24 << 20),
        cost_estimate=pl.CostEstimate(
            flops=12_000_000_000, bytes_accessed=4 << 20, transcendentals=0
        ),
        name=name,
    )(*inputs)


HALF = SEC // 2


def weight_kernel(first, el_ref, er_ref, op_ref, after_ref, lower_ref, w_ref, bde, stack, b_ref, sems):
    copies = [
        pltpu.make_async_copy(lower_ref.at[first + s], b_ref.at[s], sems.at[s]) for s in range(HALF)
    ]
    for copy in copies:
        copy.start()
    bde[...] = jnp.zeros_like(bde)
    spread = jnp.where(iota2((WIDE, KM), 0) // 16 == iota2((WIDE, KM), 1), 1.0, 0.0).astype(BF16)
    same = iota2((WIDE, WIDE), 0) % 16 == iota2((WIDE, WIDE), 1) % 16
    for copy in copies:
        copy.wait()

    both = {}
    for s in range(HALF):
        for g in range(GROUPS):
            at = slice(g * PAD, (g + 1) * PAD)
            bde[s, at, at] = er_ref[first + s]
    uppers = [mm(el_ref[first + s], b_ref[s]).astype(BF16) for s in range(HALF)]
    for s in range(HALF):
        for g in range(4):
            both[s, g] = mmt(uppers[s][:, g * WIDE : (g + 1) * WIDE], bde[s]).astype(BF16)
    for s in range(HALF):
        for l in range(KM):
            i = l % 4
            for h in range(GROUPS):
                stack[s, l * 16 : (l + 1) * 16, h * PAD : (h + 1) * PAD] = both[s, l // 4][
                    h * 16 : (h + 1) * 16, i * PAD : (i + 1) * PAD
                ]
    pairs = [(q, s) for s in range(HALF) for q in range(2)]
    spreads = [mm(spread, op_ref[q, first + s]).astype(BF16) for q, s in pairs]
    grown = [jnp.where(same, mmt(rows, spread), 0.0).astype(BF16) for rows in spreads]
    for (q, s), matrix in zip(pairs, grown):
        out = mm(matrix, stack[s]).astype(BF16)
        for k in range(KM):
            for h in range(GROUPS):
                w_ref[q, s, h * 16 : (h + 1) * 16, k * PAD : (k + 1) * PAD] = out[
                    k * 16 : (k + 1) * 16, h * PAD : (h + 1) * PAD
                ]


def observable_weights(first, lower, left_env, right_env, operators, after):
    return pl.pallas_call(
        lambda *refs: weight_kernel(first, *refs),
        out_shape=jax.ShapeDtypeStruct((2, HALF, PAD, SITE), BF16),
        in_specs=vmem(3) + anywhere(2),
        out_specs=vmem(1)[0],
        scratch_shapes=[
            pltpu.VMEM((HALF, WIDE, WIDE), BF16),
            pltpu.VMEM((HALF, WIDE, WIDE), BF16),
            pltpu.VMEM((HALF, PAD, SITE), BF16),
            pltpu.SemaphoreType.DMA((HALF,)),
        ],
        compiler_params=pltpu.CompilerParams(vmem_limit_bytes=16 << 20),
        cost_estimate=pl.CostEstimate(
            flops=3_000_000_000, bytes_accessed=2 << 20, transcendentals=0
        ),
        name="observable_weights",
    )(left_env, right_env, operators, after, lower)


def finish_kernel(entries, g_ref, *refs):
    *refs, low_ref, high_ref, out_ref, log_ref, obs_ref = refs
    us = refs
    row, col = lax.axis_index("row"), lax.axis_index("col")
    columns = g_ref.shape[0] // ROWS
    at_s = iota2((1, SEC), 1)
    at_qs, at_q = iota2((2, SEC), 1), iota2((2, SEC), 0)
    logs = jnp.zeros((1, SEC), F32)
    factors = []
    for i in range(ROWS):
        for k in range(2):
            scale = jnp.ones((columns, 1), F32)
            factor = jnp.zeros((columns, 1), F32)
            log = jnp.zeros((1, 1), F32)
            here = pl.ds(i * columns, columns)
            for r in range(ROWS):
                lane = 2 * ROWS * k + 2 * r
                squares = scale * scale * g_ref[here, lane + 1 : lane + 2]
                norm = jnp.sqrt(jnp.sum(squares, axis=0, keepdims=True) / entries + epsilon)
                scale = scale / norm
                factor = jnp.where(row == r, scale, factor)
                log = jnp.where(row == r, jnp.log(norm), log)
                scale = scale * g_ref[here, lane : lane + 1]
            at_col = iota2((columns, 1), 0) == col
            factors.append(jnp.sum(jnp.where(at_col, factor, 0.0), axis=0, keepdims=True))
            logs = jnp.where(at_s == 2 * i + k, log, logs)
    log_ref[...] = logs
    values = jnp.zeros((2, SEC), F32)
    for k in range(2):
        for x in range(ROWS):
            i = row ^ x
            s = 2 * i + k
            upper_half = i >= ROWS // 2
            at = s - jnp.where(upper_half, HALF, 0)
            factor = factors[k]
            for other in range(1, ROWS):
                factor = jnp.where(i == other, factors[2 * other + k], factor)
            u = us[x][k].astype(F32) * factor
            out_ref[s] = u.astype(BF16)
            for q in range(2):
                w = jnp.where(upper_half, high_ref[q, at].astype(F32), low_ref[q, at].astype(F32))
                value = total(u * w)
                values = jnp.where((at_q == q) & (at_qs == s), value, values)
    obs_ref[...] = values / math.sqrt(KM)


def finish(entries, gathered, weights, us):
    return pl.pallas_call(
        lambda *refs: finish_kernel(entries, *refs),
        out_shape=(
            jax.ShapeDtypeStruct((SEC, PAD, SITE), BF16),
            jax.ShapeDtypeStruct((1, SEC), F32),
            jax.ShapeDtypeStruct((2, SEC), F32),
        ),
        in_specs=vmem(3 + len(us)),
        out_specs=tuple(vmem(3)),
        compiler_params=pltpu.CompilerParams(vmem_limit_bytes=16 << 20),
        cost_estimate=pl.CostEstimate(flops=2_000_000, bytes_accessed=2 << 20, transcendentals=0),
        name="finish",
    )(gathered, *us, *weights)


def following(block):
    return passed_along(block, "col", -1)


def passed_along(block, axis, distance):
    devices = range(lax.axis_size(axis))
    route = [((i - distance) % len(devices), i) for i in devices]
    return lax.ppermute(block, axis, route)


def exchanged(block, x):
    return lax.ppermute(block, "row", [(i, i ^ x) for i in range(ROWS)])


NEAR_FIRST = (1, 3, 2)


def exchanged_all(blocks):
    got = {x: exchanged(blocks[x], x) for x in NEAR_FIRST}
    return [blocks[0]] + [got[x] for x in range(1, ROWS)]


def on_device(
    top_boundary, row_transfer, proj_in, proj_out, bottom_boundary, environments, operators, ranks
):
    columns = lax.axis_size("col")
    envs = environments[0, 0]
    lefts, transfers = proj_in[0, 0], row_transfer[0, 0]
    perm = bond_swap()
    lower = bottom_boundary[0, 0]
    *packed, q1, q2 = pack(0, ranks, lefts, transfers, ranks, proj_out[0, 0])
    pts1 = exchanged_all(packed)
    next1, next2, next_envs = following(q1), following(q2), following(envs)
    rights = mask_rights(ranks, ranks, next1)
    qs1 = exchanged_all(rights)
    packed = pack(1, ranks, lefts, transfers, rights[0], next2)
    ptqs2 = exchanged_all(packed)
    low = observable_weights(0, lower, envs, next_envs, operators, packed[0])
    top = top_boundary[0]
    *us1, stats = chain(pts1, qs1, top, perm, None, (), low, 8, "chain_first")
    high = observable_weights(HALF, lower, envs, next_envs, operators, stats)
    everyone = ROWS * columns
    *us, stats = chain(ptqs2, None, top, perm, stats, us1, high, everyone, "chain_second")
    us = exchanged_all(us)
    gathered = lax.all_to_all(stats, ("row", "col"), 0, 0, tiled=True)
    entries = float(columns * PAD * KM * PAD)
    sites, logs, values = finish(entries, gathered, (low, high), us)
    return sites[None, None], logs, values[:, None, None]


def solution(mesh):
    in_specs = (
        P("col", None, None, None),
        P("row", "col", None, None, None),
        P("row", "col", None, None, None),
        P("row", "col", None, None, None),
        P("row", "col", None, None, None),
        P("row", "col", None, None, None),
        P(),
        P("row", None),
    )
    out_specs = (P("row", "col", None, None, None), P("row", None), P(None, "row", "col", None))
    return jax.shard_map(
        on_device, mesh=mesh, in_specs=in_specs, out_specs=out_specs, check_vma=False
    )
```

```python
import math

import jax
import jax.numpy as jnp
import numpy as np
from jax import lax
from jax.experimental import pallas as pl
from jax.experimental.pallas import tpu as pltpu
from jax.sharding import PartitionSpec as P

SEC = 8
PAD = 64
KM = 16
DB = 16
ROWS = 4
WIDE = 256
GROUPS = WIDE // PAD
SITE = KM * PAD
LANES = 128

BF16 = jnp.bfloat16
F32 = jnp.float32

epsilon = 1e-06


def mm(a, b):
    return jnp.dot(a, b, preferred_element_type=F32)


def mmt(a, b):
    return lax.dot_general(a, b, (((1,), (1,)), ((), ())), preferred_element_type=F32)


def iota2(shape, dim):
    return lax.broadcasted_iota(jnp.int32, shape, dim)


def digit_swap():
    i, j = iota2((WIDE, WIDE), 0), iota2((WIDE, WIDE), 1)
    return jnp.where((i // 16 == j % 16) & (i % 16 == j // 16), 1.0, 0.0).astype(BF16)


def bond_swap():
    i = np.arange(SITE)
    matrix = np.zeros((SITE, SITE), np.float32)
    matrix[i, (i % DB) * PAD + i // DB] = 1.0
    return jnp.asarray(matrix, BF16)


def total(x):
    return jnp.sum(jnp.sum(x, axis=1, keepdims=True), axis=0, keepdims=True)


def vmem(count):
    return [pl.BlockSpec(memory_space=pltpu.VMEM)] * count


def smem():
    return pl.BlockSpec(memory_space=pltpu.SMEM)


def masked(block, inside):
    return jnp.where(inside, block.astype(F32), 0.0).astype(BF16)


def anywhere(count):
    return [pl.BlockSpec(memory_space=pl.ANY)] * count


def params(mib):
    return pltpu.CompilerParams(vmem_limit_bytes=mib << 20)


def light(mib):
    return pl.CostEstimate(flops=1_000_000, bytes_accessed=mib << 20, transcendentals=0)


ENV = PAD // 2


def env_lanes(s, h):
    return slice((h * SEC + s) * PAD, (h * SEC + s + 1) * PAD)


def pack_kernel(k, rank_ref, p_ref, t_ref, after_ref, *refs):
    rights, raws = (), ()
    if k == 0:
        q_ref, env_ref, *refs = refs
        outs, raws = refs[:ROWS], refs[ROWS : ROWS + 2]
        held, env, sems = refs[ROWS + 2 :]
        bring = pltpu.make_async_copy(env_ref, env, sems.at[4, 0])
        bring.start()
    else:
        *rights, outs, held, sems = refs[0], refs[1 : ROWS + 1], refs[ROWS + 1], refs[ROWS + 2]
    me = lax.axis_index("row")
    at = iota2((PAD, WIDE), 0)
    copies = []
    for x in range(ROWS):
        s = 2 * (me ^ x) + k
        copies.append(
            (
                pltpu.make_async_copy(p_ref.at[s], held.at[x], sems.at[0, x]),
                pltpu.make_async_copy(t_ref.at[s], outs[x].at[1], sems.at[1, x]),
            )
        )
    picks = [
        pltpu.make_async_copy(
            q_ref.at[2 * (me ^ x) + j], raws[j].at[pl.ds(x * PAD, PAD)], sems.at[2 + j, x]
        )
        for j in range(len(raws))
        for x in range(ROWS)
    ]
    for pair in copies:
        for copy in pair:
            copy.start()
    for copy in picks:
        copy.start()
    for x in range(ROWS):
        inside = at < rank_ref[0, 2 * (me ^ x) + k]
        copies[x][0].wait()
        for g in range(GROUPS):
            rows, lanes = slice(g * PAD, (g + 1) * PAD), slice(g * WIDE, (g + 1) * WIDE)
            outs[x][0, rows, :] = masked(held[x, :, lanes], inside)
            if k == 1:
                outs[x][2, rows, :] = masked(
                    rights[0][x * PAD : (x + 1) * PAD, lanes], inside
                )
    for x in range(ROWS):
        copies[x][1].wait()
    if k == 0:
        bring.wait()
        for s in range(SEC):
            for h in range(2):
                raws[0][ROWS * PAD :, env_lanes(s, h)] = env[s, h * ENV : (h + 1) * ENV, :]
    for copy in picks:
        copy.wait()


def pack(k, ranks, p, t, after, *rights):
    raws, env = (), []
    if k == 0:
        raws = tuple(
            jax.ShapeDtypeStruct((ROWS * PAD + extra, SITE), BF16) for extra in (ENV, 0)
        )
        env = [pltpu.VMEM((SEC, PAD, PAD), BF16)]
    return pl.pallas_call(
        lambda *refs: pack_kernel(k, *refs),
        out_shape=(jax.ShapeDtypeStruct((2 + k, WIDE, WIDE), BF16),) * ROWS + raws,
        in_specs=[smem()] + anywhere(3) + (vmem(1) if k else anywhere(2)),
        out_specs=tuple(vmem(ROWS + len(raws))),
        scratch_shapes=[
            pltpu.VMEM((ROWS, PAD, SITE), BF16),
            *env,
            pltpu.SemaphoreType.DMA((5, ROWS)),
        ],
        compiler_params=params(8 if k else 56),
        cost_estimate=light(2),
        name="pack_second" if k else "pack_first",
    )(ranks, p, t, after, *rights)


def mask_rights_kernel(rank_ref, after_ref, q_ref, *outs):
    me = lax.axis_index("row")
    at = iota2((PAD, WIDE), 0)
    for x in range(ROWS):
        inside = at < rank_ref[0, 2 * (me ^ x)]
        for g in range(GROUPS):
            rows, lanes = slice(g * PAD, (g + 1) * PAD), slice(g * WIDE, (g + 1) * WIDE)
            outs[x][rows, :] = masked(q_ref[x * PAD : (x + 1) * PAD, lanes], inside)


def mask_rights(ranks, after, q):
    return pl.pallas_call(
        mask_rights_kernel,
        out_shape=(jax.ShapeDtypeStruct((WIDE, WIDE), BF16),) * ROWS,
        in_specs=[smem()] + anywhere(1) + vmem(1),
        out_specs=tuple(vmem(ROWS)),
        compiler_params=params(8),
        cost_estimate=light(1),
        name="mask_rights",
    )(ranks, after, q)


def chain_kernel(
    pts, qs, m_ref, perm_ref, before_ref, befores, us, st_ref,
    bdm, bdq, xs, ys, qw, pw, lefts, middles, stack, site, place, zs, held, sem,
):
    me = lax.axis_index("row")
    k0 = len(befores) // ROWS
    start = pltpu.make_async_copy(m_ref.at[2 * me + k0], site, sem)
    start.start()
    swap = digit_swap()
    bdm[...] = jnp.zeros_like(bdm)
    bdq[...] = jnp.zeros_like(bdq)
    for pieces, dst in (([ref.at[0] for ref in pts], pw), (qs, qw)):
        acc = None
        for part in range(GROUPS):
            rows = jnp.concatenate([ref[part * PAD : (part + 1) * PAD, :] for ref in pieces], axis=0)
            term = mm(rows, perm_ref[part * WIDE : (part + 1) * WIDE, :])
            acc = term if acc is None else acc + term
        dst[...] = acc.astype(BF16)
    for x in range(ROWS):
        for w in range(DB):
            for g in range(GROUPS):
                stack[x, w * 16 : (w + 1) * 16, g * PAD : (g + 1) * PAD] = pw[
                    x * PAD + g * 16 : x * PAD + (g + 1) * 16, w * PAD : (w + 1) * PAD
                ]
    for x in range(ROWS):
        lefts[me ^ x] = mm(swap, stack[x]).astype(BF16)
        middles[me ^ x] = mm(mmt(swap, pts[x][1]).astype(BF16), swap).astype(BF16)
    start.wait()
    for x in range(len(befores)):
        us[x][0] = befores[x][0]
    lane = iota2((1, LANES), 1)
    stats = jnp.zeros((1, LANES), F32)
    inverse = None
    for r in range(ROWS):
        base = pl.multiple_of((me ^ r) * PAD, PAD)
        left, middle = lefts[r], middles[r]
        for k in range(KM):
            lanes = slice(k * PAD, (k + 1) * PAD)
            right = qw[pl.ds(base, PAD), lanes]
            for g in range(GROUPS):
                at = slice(g * PAD, (g + 1) * PAD)
                if r == 0:
                    bdm[k, at, at] = site[:, lanes]
                else:
                    for h in range(GROUPS):
                        bdm[k, g * PAD + h * 16 : g * PAD + (h + 1) * 16, at] = place[
                            k * 16 : (k + 1) * 16, h * PAD : (h + 1) * PAD
                        ]
                bdq[r % 2, at, k * WIDE + g * PAD : k * WIDE + (g + 1) * PAD] = right
            first = mm(left, bdm[k]).astype(BF16)
            xs[:, k * 16 : (k + 1) * 16, :] = first.reshape(16, 16, WIDE)
        for c in range(16):
            second = mm(middle, xs[c]).astype(BF16)
            for e in range(DB):
                ys[c * 16 : (c + 1) * 16, e * WIDE : (e + 1) * WIDE] = second[e * 16 : (e + 1) * 16]
            if r > 0:
                for g in range(GROUPS):
                    held[r - 1, g * 16 : (g + 1) * 16, c * PAD : (c + 1) * PAD] = place[
                        c * 16 : (c + 1) * 16, g * PAD : (g + 1) * PAD
                    ]

        @pl.when(me >= 0)
        def _(r=r):
            zs[...] = mmt(ys[...], bdq[r % 2])

        z = zs[...]
        if inverse is not None:
            z = z * inverse
        place[...] = mm(swap, z.astype(BF16)).astype(BF16)
        top = jnp.max(jnp.max(jnp.abs(z), axis=1, keepdims=True), axis=0, keepdims=True)
        top = jnp.where(top > 0, top, 1.0)
        inverse = 1.0 / top
        stats = jnp.where(lane == 2 * r, top, stats)
        stats = jnp.where(lane == 2 * r + 1, total(z * z), stats)
    for c in range(KM):
        for g in range(GROUPS):
            held[ROWS - 1, g * 16 : (g + 1) * 16, c * PAD : (c + 1) * PAD] = place[
                c * 16 : (c + 1) * 16, g * PAD : (g + 1) * PAD
            ]
    for x in range(ROWS):
        us[x][k0] = held[me ^ x]
    if befores:
        stats = jnp.where(lane < 2 * ROWS, before_ref[0:1, :], pltpu.roll(stats, 2 * ROWS, 1))
    st_ref[...] = jnp.broadcast_to(stats, st_ref.shape)


def chain(pts, qs, m, perm, before, befores, after, copies, name):
    inputs = [*pts, *(qs or ()), perm, *([before] if befores else []), *befores, after, m]
    sites = 2 if befores else 1

    def body(*refs):
        pt_refs, refs = refs[:ROWS], refs[ROWS:]
        if qs is None:
            q_refs = [ref.at[2] for ref in pt_refs]
        else:
            q_refs, refs = refs[:ROWS], refs[ROWS:]
        perm_ref, *refs = refs
        before_ref = None
        if befores:
            before_ref, *refs = refs
        before_sites, refs = refs[: len(befores)], refs[len(befores) :]
        _, m_ref, *refs = refs
        us, (st_ref, *scratch) = refs[:ROWS], refs[ROWS:]
        chain_kernel(
            pt_refs, q_refs, m_ref, perm_ref, before_ref, before_sites, us, st_ref, *scratch
        )

    site = jax.ShapeDtypeStruct((sites, PAD, SITE), BF16)
    return pl.pallas_call(
        body,
        out_shape=(site,) * ROWS + (jax.ShapeDtypeStruct((copies, LANES), F32),),
        in_specs=vmem(len(inputs) - 2) + anywhere(2),
        out_specs=tuple(vmem(ROWS + 1)),
        scratch_shapes=[
            pltpu.VMEM((KM, WIDE, WIDE), BF16),
            pltpu.VMEM((2, WIDE, DB * WIDE), BF16),
            pltpu.VMEM((16, WIDE, WIDE), BF16),
            pltpu.VMEM((WIDE, DB * WIDE), BF16),
            pltpu.VMEM((ROWS * PAD, SITE), BF16),
            pltpu.VMEM((ROWS * PAD, SITE), BF16),
            pltpu.VMEM((ROWS, WIDE, WIDE), BF16),
            pltpu.VMEM((ROWS, WIDE, WIDE), BF16),
            pltpu.VMEM((ROWS, WIDE, WIDE), BF16),
            pltpu.VMEM((PAD, SITE), BF16),
            pltpu.VMEM((WIDE, WIDE), BF16),
            pltpu.VMEM((WIDE, WIDE), F32),
            pltpu.VMEM((ROWS, PAD, SITE), BF16),
            pltpu.SemaphoreType.DMA,
        ],
        compiler_params=pltpu.CompilerParams(vmem_limit_bytes=24 << 20),
        cost_estimate=pl.CostEstimate(
            flops=12_000_000_000, bytes_accessed=4 << 20, transcendentals=0
        ),
        name=name,
    )(*inputs)


HALF = SEC // 2


def weight_kernel(first, el_ref, er_ref, op_ref, after_ref, lower_ref, w_ref, bde, stack, b_ref, sems):
    copies = [
        pltpu.make_async_copy(lower_ref.at[first + s], b_ref.at[s], sems.at[s]) for s in range(HALF)
    ]
    for copy in copies:
        copy.start()
    bde[...] = jnp.zeros_like(bde)
    spread = jnp.where(iota2((WIDE, KM), 0) // 16 == iota2((WIDE, KM), 1), 1.0, 0.0).astype(BF16)
    same = iota2((WIDE, WIDE), 0) % 16 == iota2((WIDE, WIDE), 1) % 16
    for copy in copies:
        copy.wait()

    both = {}
    for s in range(HALF):
        for g in range(GROUPS):
            at = slice(g * PAD, (g + 1) * PAD)
            for h in range(2):
                half = slice(g * PAD + h * ENV, g * PAD + (h + 1) * ENV)
                bde[s, half, at] = er_ref[ROWS * PAD :, env_lanes(first + s, h)]
    uppers = [mm(el_ref[first + s], b_ref[s]).astype(BF16) for s in range(HALF)]
    for s in range(HALF):
        for g in range(4):
            both[s, g] = mmt(uppers[s][:, g * WIDE : (g + 1) * WIDE], bde[s]).astype(BF16)
    for s in range(HALF):
        for l in range(KM):
            i = l % 4
            for h in range(GROUPS):
                stack[s, l * 16 : (l + 1) * 16, h * PAD : (h + 1) * PAD] = both[s, l // 4][
                    h * 16 : (h + 1) * 16, i * PAD : (i + 1) * PAD
                ]
    pairs = [(q, s) for s in range(HALF) for q in range(2)]
    spreads = [mm(spread, op_ref[q, first + s]).astype(BF16) for q, s in pairs]
    grown = [jnp.where(same, mmt(rows, spread), 0.0).astype(BF16) for rows in spreads]
    for (q, s), matrix in zip(pairs, grown):
        out = mm(matrix, stack[s]).astype(BF16)
        for k in range(KM):
            for h in range(GROUPS):
                w_ref[q, s, h * 16 : (h + 1) * 16, k * PAD : (k + 1) * PAD] = out[
                    k * 16 : (k + 1) * 16, h * PAD : (h + 1) * PAD
                ]


def observable_weights(first, lower, left_env, right_env, operators, after):
    return pl.pallas_call(
        lambda *refs: weight_kernel(first, *refs),
        out_shape=jax.ShapeDtypeStruct((2, HALF, PAD, SITE), BF16),
        in_specs=vmem(3) + anywhere(2),
        out_specs=vmem(1)[0],
        scratch_shapes=[
            pltpu.VMEM((HALF, WIDE, WIDE), BF16),
            pltpu.VMEM((HALF, WIDE, WIDE), BF16),
            pltpu.VMEM((HALF, PAD, SITE), BF16),
            pltpu.SemaphoreType.DMA((HALF,)),
        ],
        compiler_params=pltpu.CompilerParams(vmem_limit_bytes=16 << 20),
        cost_estimate=pl.CostEstimate(
            flops=3_000_000_000, bytes_accessed=2 << 20, transcendentals=0
        ),
        name="observable_weights",
    )(left_env, right_env, operators, after, lower)


def finish_kernel(entries, g_ref, *refs):
    *refs, low_ref, high_ref, out_ref, log_ref, obs_ref = refs
    us = refs
    row, col = lax.axis_index("row"), lax.axis_index("col")
    columns = g_ref.shape[0] // ROWS
    at_s = iota2((1, SEC), 1)
    at_qs, at_q = iota2((2, SEC), 1), iota2((2, SEC), 0)
    logs = jnp.zeros((1, SEC), F32)
    factors = []
    for i in range(ROWS):
        for k in range(2):
            scale = jnp.ones((columns, 1), F32)
            factor = jnp.zeros((columns, 1), F32)
            log = jnp.zeros((1, 1), F32)
            here = pl.ds(i * columns, columns)
            for r in range(ROWS):
                lane = 2 * ROWS * k + 2 * r
                squares = scale * scale * g_ref[here, lane + 1 : lane + 2]
                norm = jnp.sqrt(jnp.sum(squares, axis=0, keepdims=True) / entries + epsilon)
                scale = scale / norm
                factor = jnp.where(row == r, scale, factor)
                log = jnp.where(row == r, jnp.log(norm), log)
                scale = scale * g_ref[here, lane : lane + 1]
            at_col = iota2((columns, 1), 0) == col
            factors.append(jnp.sum(jnp.where(at_col, factor, 0.0), axis=0, keepdims=True))
            logs = jnp.where(at_s == 2 * i + k, log, logs)
    log_ref[...] = logs
    values = jnp.zeros((2, SEC), F32)
    for k in range(2):
        for x in range(ROWS):
            i = row ^ x
            s = 2 * i + k
            upper_half = i >= ROWS // 2
            at = s - jnp.where(upper_half, HALF, 0)
            factor = factors[k]
            for other in range(1, ROWS):
                factor = jnp.where(i == other, factors[2 * other + k], factor)
            u = us[x][k].astype(F32) * factor
            out_ref[s] = u.astype(BF16)
            for q in range(2):
                w = jnp.where(upper_half, high_ref[q, at].astype(F32), low_ref[q, at].astype(F32))
                value = total(u * w)
                values = jnp.where((at_q == q) & (at_qs == s), value, values)
    obs_ref[...] = values / math.sqrt(KM)


def finish(entries, gathered, weights, us):
    return pl.pallas_call(
        lambda *refs: finish_kernel(entries, *refs),
        out_shape=(
            jax.ShapeDtypeStruct((SEC, PAD, SITE), BF16),
            jax.ShapeDtypeStruct((1, SEC), F32),
            jax.ShapeDtypeStruct((2, SEC), F32),
        ),
        in_specs=vmem(3 + len(us)),
        out_specs=tuple(vmem(3)),
        compiler_params=pltpu.CompilerParams(vmem_limit_bytes=16 << 20),
        cost_estimate=pl.CostEstimate(flops=2_000_000, bytes_accessed=2 << 20, transcendentals=0),
        name="finish",
    )(gathered, *us, *weights)


def following(block):
    return passed_along(block, "col", -1)


def passed_along(block, axis, distance):
    devices = range(lax.axis_size(axis))
    route = [((i - distance) % len(devices), i) for i in devices]
    return lax.ppermute(block, axis, route)


def exchanged(block, x):
    return lax.ppermute(block, "row", [(i, i ^ x) for i in range(ROWS)])


NEAR_FIRST = (1, 3, 2)


def exchanged_all(blocks):
    got = {x: exchanged(blocks[x], x) for x in NEAR_FIRST}
    return [blocks[0]] + [got[x] for x in range(1, ROWS)]


def on_device(
    top_boundary, row_transfer, proj_in, proj_out, bottom_boundary, environments, operators, ranks
):
    columns = lax.axis_size("col")
    envs = environments[0, 0]
    lefts, transfers = proj_in[0, 0], row_transfer[0, 0]
    perm = bond_swap()
    lower = bottom_boundary[0, 0]
    *packed, q1, q2 = pack(0, ranks, lefts, transfers, ranks, proj_out[0, 0], envs)
    pts1 = exchanged_all(packed)
    next1, next2 = following(q1), following(q2)
    rights = mask_rights(ranks, ranks, next1)
    qs1 = exchanged_all(rights)
    low = observable_weights(0, lower, envs, next1, operators, rights[0])
    packed = pack(1, ranks, lefts, transfers, low, next2)
    ptqs2 = exchanged_all(packed)
    top = top_boundary[0]
    *us1, stats = chain(pts1, qs1, top, perm, None, (), packed[0], 8, "chain_first")
    high = observable_weights(HALF, lower, envs, next1, operators, stats)
    everyone = ROWS * columns
    *us, stats = chain(ptqs2, None, top, perm, stats, us1, high, everyone, "chain_second")
    us = exchanged_all(us)
    gathered = lax.all_to_all(stats, ("row", "col"), 0, 0, tiled=True)
    entries = float(columns * PAD * KM * PAD)
    sites, logs, values = finish(entries, gathered, (low, high), us)
    return sites[None, None], logs, values[:, None, None]


def solution(mesh):
    in_specs = (
        P("col", None, None, None),
        P("row", "col", None, None, None),
        P("row", "col", None, None, None),
        P("row", "col", None, None, None),
        P("row", "col", None, None, None),
        P("row", "col", None, None, None),
        P(),
        P("row", None),
    )
    out_specs = (P("row", "col", None, None, None), P("row", None), P(None, "row", "col", None))
    return jax.shard_map(
        on_device, mesh=mesh, in_specs=in_specs, out_specs=out_specs, check_vma=False
    )
```

```python
import math

import jax
import jax.numpy as jnp
import numpy as np
from jax import lax
from jax.experimental import pallas as pl
from jax.experimental.pallas import tpu as pltpu
from jax.sharding import PartitionSpec as P

SEC = 8
PAD = 64
KM = 16
DB = 16
ROWS = 4
WIDE = 256
GROUPS = WIDE // PAD
SITE = KM * PAD
LANES = 128

BF16 = jnp.bfloat16
F32 = jnp.float32

epsilon = 1e-06


def mm(a, b):
    return jnp.dot(a, b, preferred_element_type=F32)


def mmt(a, b):
    return lax.dot_general(a, b, (((1,), (1,)), ((), ())), preferred_element_type=F32)


def iota2(shape, dim):
    return lax.broadcasted_iota(jnp.int32, shape, dim)


def digit_swap():
    i, j = iota2((WIDE, WIDE), 0), iota2((WIDE, WIDE), 1)
    return jnp.where((i // 16 == j % 16) & (i % 16 == j // 16), 1.0, 0.0).astype(BF16)


def bond_swap():
    i = np.arange(SITE)
    matrix = np.zeros((SITE, SITE), np.float32)
    matrix[i, (i % DB) * PAD + i // DB] = 1.0
    return jnp.asarray(matrix, BF16)


def total(x):
    return jnp.sum(jnp.sum(x, axis=1, keepdims=True), axis=0, keepdims=True)


def vmem(count):
    return [pl.BlockSpec(memory_space=pltpu.VMEM)] * count


def smem():
    return pl.BlockSpec(memory_space=pltpu.SMEM)


def masked(block, inside):
    return jnp.where(inside, block.astype(F32), 0.0).astype(BF16)


def anywhere(count):
    return [pl.BlockSpec(memory_space=pl.ANY)] * count


def params(mib):
    return pltpu.CompilerParams(vmem_limit_bytes=mib << 20)


def light(mib):
    return pl.CostEstimate(flops=1_000_000, bytes_accessed=mib << 20, transcendentals=0)


ENV = PAD // 2


def env_lanes(s, h):
    return slice((h * SEC + s) * PAD, (h * SEC + s + 1) * PAD)


def pack_kernel(k, rank_ref, p_ref, t_ref, after_ref, *refs):
    rights, raws = (), ()
    if k == 0:
        q_ref, env_ref, *refs = refs
        outs, raws = refs[:ROWS], refs[ROWS : ROWS + 2]
        held, env, sems = refs[ROWS + 2 :]
        bring = pltpu.make_async_copy(env_ref, env, sems.at[4, 0])
        bring.start()
    else:
        *rights, outs, held, sems = refs[0], refs[1 : ROWS + 1], refs[ROWS + 1], refs[ROWS + 2]
    me = lax.axis_index("row")
    at = iota2((PAD, WIDE), 0)
    copies = []
    for x in range(ROWS):
        s = 2 * (me ^ x) + k
        copies.append(
            (
                pltpu.make_async_copy(p_ref.at[s], held.at[x], sems.at[0, x]),
                pltpu.make_async_copy(t_ref.at[s], outs[x].at[1], sems.at[1, x]),
            )
        )
    picks = [
        pltpu.make_async_copy(
            q_ref.at[2 * (me ^ x) + j], raws[j].at[pl.ds(x * PAD, PAD)], sems.at[2 + j, x]
        )
        for j in range(len(raws))
        for x in range(ROWS)
    ]
    for pair in copies:
        for copy in pair:
            copy.start()
    for copy in picks:
        copy.start()
    for x in range(ROWS):
        inside = at < rank_ref[0, 2 * (me ^ x) + k]
        copies[x][0].wait()
        for g in range(GROUPS):
            rows, lanes = slice(g * PAD, (g + 1) * PAD), slice(g * WIDE, (g + 1) * WIDE)
            outs[x][0, rows, :] = masked(held[x, :, lanes], inside)
            if k == 1:
                outs[x][2, rows, :] = masked(
                    rights[0][x * PAD : (x + 1) * PAD, lanes], inside
                )
    for x in range(ROWS):
        copies[x][1].wait()
    if k == 0:
        bring.wait()
        for s in range(SEC):
            for h in range(2):
                raws[0][ROWS * PAD :, env_lanes(s, h)] = env[s, h * ENV : (h + 1) * ENV, :]
    for copy in picks:
        copy.wait()


def pack(k, ranks, p, t, after, *rights):
    raws, env = (), []
    if k == 0:
        raws = tuple(
            jax.ShapeDtypeStruct((ROWS * PAD + extra, SITE), BF16) for extra in (ENV, 0)
        )
        env = [pltpu.VMEM((SEC, PAD, PAD), BF16)]
    return pl.pallas_call(
        lambda *refs: pack_kernel(k, *refs),
        out_shape=(jax.ShapeDtypeStruct((2 + k, WIDE, WIDE), BF16),) * ROWS + raws,
        in_specs=[smem()] + anywhere(3) + (vmem(1) if k else anywhere(2)),
        out_specs=tuple(vmem(ROWS + len(raws))),
        scratch_shapes=[
            pltpu.VMEM((ROWS, PAD, SITE), BF16),
            *env,
            pltpu.SemaphoreType.DMA((5, ROWS)),
        ],
        compiler_params=params(8 if k else 56),
        cost_estimate=light(2),
        name="pack_second" if k else "pack_first",
    )(ranks, p, t, after, *rights)


def mask_rights_kernel(rank_ref, after_ref, q_ref, *outs):
    me = lax.axis_index("row")
    at = iota2((PAD, WIDE), 0)
    for x in range(ROWS):
        inside = at < rank_ref[0, 2 * (me ^ x)]
        for g in range(GROUPS):
            rows, lanes = slice(g * PAD, (g + 1) * PAD), slice(g * WIDE, (g + 1) * WIDE)
            outs[x][rows, :] = masked(q_ref[x * PAD : (x + 1) * PAD, lanes], inside)


def mask_rights(ranks, after, q):
    return pl.pallas_call(
        mask_rights_kernel,
        out_shape=(jax.ShapeDtypeStruct((WIDE, WIDE), BF16),) * ROWS,
        in_specs=[smem()] + anywhere(1) + vmem(1),
        out_specs=tuple(vmem(ROWS)),
        compiler_params=params(8),
        cost_estimate=light(1),
        name="mask_rights",
    )(ranks, after, q)


def chain_kernel(
    pts, qs, m_ref, perm_ref, before_ref, befores, us, st_ref,
    bdm, bdq, xs, ys, qw, pw, lefts, middles, stack, site, place, zs, held, sem,
):
    me = lax.axis_index("row")
    k0 = len(befores) // ROWS
    start = pltpu.make_async_copy(m_ref.at[2 * me + k0], site, sem)
    start.start()
    swap = digit_swap()
    bdm[...] = jnp.zeros_like(bdm)
    bdq[...] = jnp.zeros_like(bdq)
    for pieces, dst in (([ref.at[0] for ref in pts], pw), (qs, qw)):
        acc = None
        for part in range(GROUPS):
            rows = jnp.concatenate([ref[part * PAD : (part + 1) * PAD, :] for ref in pieces], axis=0)
            term = mm(rows, perm_ref[part * WIDE : (part + 1) * WIDE, :])
            acc = term if acc is None else acc + term
        dst[...] = acc.astype(BF16)
    for x in range(ROWS):
        for w in range(DB):
            for g in range(GROUPS):
                stack[x, w * 16 : (w + 1) * 16, g * PAD : (g + 1) * PAD] = pw[
                    x * PAD + g * 16 : x * PAD + (g + 1) * 16, w * PAD : (w + 1) * PAD
                ]
    for x in range(ROWS):
        lefts[me ^ x] = mm(swap, stack[x]).astype(BF16)
        middles[me ^ x] = mm(mmt(swap, pts[x][1]).astype(BF16), swap).astype(BF16)
    start.wait()
    for x in range(len(befores)):
        us[x][0] = befores[x][0]
    lane = iota2((1, LANES), 1)
    stats = jnp.zeros((1, LANES), F32)
    inverse = None
    for r in range(ROWS):
        base = pl.multiple_of((me ^ r) * PAD, PAD)
        left, middle = lefts[r], middles[r]
        for k in range(KM):
            lanes = slice(k * PAD, (k + 1) * PAD)
            right = qw[pl.ds(base, PAD), lanes]
            for g in range(GROUPS):
                at = slice(g * PAD, (g + 1) * PAD)
                if r == 0:
                    bdm[k, at, at] = site[:, lanes]
                else:
                    for h in range(GROUPS):
                        bdm[k, g * PAD + h * 16 : g * PAD + (h + 1) * 16, at] = place[
                            k * 16 : (k + 1) * 16, h * PAD : (h + 1) * PAD
                        ]
                bdq[at, k * WIDE + g * PAD : k * WIDE + (g + 1) * PAD] = right
            first = mm(left, bdm[k]).astype(BF16)
            xs[:, k * 16 : (k + 1) * 16, :] = first.reshape(16, 16, WIDE)
        for c in range(16):
            second = mm(middle, xs[c]).astype(BF16)
            for e in range(DB):
                ys[c * 16 : (c + 1) * 16, e * WIDE : (e + 1) * WIDE] = second[e * 16 : (e + 1) * 16]
            if r > 0:
                for g in range(GROUPS):
                    held[r - 1, g * 16 : (g + 1) * 16, c * PAD : (c + 1) * PAD] = place[
                        c * 16 : (c + 1) * 16, g * PAD : (g + 1) * PAD
                    ]

        @pl.when(me >= 0)
        def _():
            zs[...] = mmt(ys[...], bdq[...])

        z = zs[...]
        if inverse is not None:
            z = z * inverse
        place[...] = mm(swap, z.astype(BF16)).astype(BF16)
        top = jnp.max(jnp.max(jnp.abs(z), axis=1, keepdims=True), axis=0, keepdims=True)
        top = jnp.where(top > 0, top, 1.0)
        inverse = 1.0 / top
        stats = jnp.where(lane == 2 * r, top, stats)
        stats = jnp.where(lane == 2 * r + 1, total(z * z), stats)
    for c in range(KM):
        for g in range(GROUPS):
            held[ROWS - 1, g * 16 : (g + 1) * 16, c * PAD : (c + 1) * PAD] = place[
                c * 16 : (c + 1) * 16, g * PAD : (g + 1) * PAD
            ]
    for x in range(ROWS):
        us[x][k0] = held[me ^ x]
    if befores:
        stats = jnp.where(lane < 2 * ROWS, before_ref[0:1, :], pltpu.roll(stats, 2 * ROWS, 1))
    st_ref[...] = jnp.broadcast_to(stats, st_ref.shape)


def chain(pts, qs, m, perm, before, befores, after, copies, name):
    inputs = [*pts, *(qs or ()), perm, *([before] if befores else []), *befores, after, m]
    sites = 2 if befores else 1

    def body(*refs):
        pt_refs, refs = refs[:ROWS], refs[ROWS:]
        if qs is None:
            q_refs = [ref.at[2] for ref in pt_refs]
        else:
            q_refs, refs = refs[:ROWS], refs[ROWS:]
        perm_ref, *refs = refs
        before_ref = None
        if befores:
            before_ref, *refs = refs
        before_sites, refs = refs[: len(befores)], refs[len(befores) :]
        _, m_ref, *refs = refs
        us, (st_ref, *scratch) = refs[:ROWS], refs[ROWS:]
        chain_kernel(
            pt_refs, q_refs, m_ref, perm_ref, before_ref, before_sites, us, st_ref, *scratch
        )

    site = jax.ShapeDtypeStruct((sites, PAD, SITE), BF16)
    return pl.pallas_call(
        body,
        out_shape=(site,) * ROWS + (jax.ShapeDtypeStruct((copies, LANES), F32),),
        in_specs=vmem(len(inputs) - 2) + anywhere(2),
        out_specs=tuple(vmem(ROWS + 1)),
        scratch_shapes=[
            pltpu.VMEM((KM, WIDE, WIDE), BF16),
            pltpu.VMEM((WIDE, DB * WIDE), BF16),
            pltpu.VMEM((16, WIDE, WIDE), BF16),
            pltpu.VMEM((WIDE, DB * WIDE), BF16),
            pltpu.VMEM((ROWS * PAD, SITE), BF16),
            pltpu.VMEM((ROWS * PAD, SITE), BF16),
            pltpu.VMEM((ROWS, WIDE, WIDE), BF16),
            pltpu.VMEM((ROWS, WIDE, WIDE), BF16),
            pltpu.VMEM((ROWS, WIDE, WIDE), BF16),
            pltpu.VMEM((PAD, SITE), BF16),
            pltpu.VMEM((WIDE, WIDE), BF16),
            pltpu.VMEM((WIDE, WIDE), F32),
            pltpu.VMEM((ROWS, PAD, SITE), BF16),
            pltpu.SemaphoreType.DMA,
        ],
        compiler_params=pltpu.CompilerParams(vmem_limit_bytes=24 << 20),
        cost_estimate=pl.CostEstimate(
            flops=12_000_000_000, bytes_accessed=4 << 20, transcendentals=0
        ),
        name=name,
    )(*inputs)


HALF = SEC // 2


def weight_kernel(first, el_ref, er_ref, op_ref, after_ref, lower_ref, w_ref, bde, stack, b_ref, sems):
    copies = [
        pltpu.make_async_copy(lower_ref.at[first + s], b_ref.at[s], sems.at[s]) for s in range(HALF)
    ]
    for copy in copies:
        copy.start()
    bde[...] = jnp.zeros_like(bde)
    spread = jnp.where(iota2((WIDE, KM), 0) // 16 == iota2((WIDE, KM), 1), 1.0, 0.0).astype(BF16)
    same = iota2((WIDE, WIDE), 0) % 16 == iota2((WIDE, WIDE), 1) % 16
    for copy in copies:
        copy.wait()

    both = {}
    for s in range(HALF):
        for g in range(GROUPS):
            at = slice(g * PAD, (g + 1) * PAD)
            for h in range(2):
                half = slice(g * PAD + h * ENV, g * PAD + (h + 1) * ENV)
                bde[s, half, at] = er_ref[ROWS * PAD :, env_lanes(first + s, h)]
    uppers = [mm(el_ref[first + s], b_ref[s]).astype(BF16) for s in range(HALF)]
    for s in range(HALF):
        for g in range(4):
            both[s, g] = mmt(uppers[s][:, g * WIDE : (g + 1) * WIDE], bde[s]).astype(BF16)
    for s in range(HALF):
        for l in range(KM):
            i = l % 4
            for h in range(GROUPS):
                stack[s, l * 16 : (l + 1) * 16, h * PAD : (h + 1) * PAD] = both[s, l // 4][
                    h * 16 : (h + 1) * 16, i * PAD : (i + 1) * PAD
                ]
    pairs = [(q, s) for s in range(HALF) for q in range(2)]
    spreads = [mm(spread, op_ref[q, first + s]).astype(BF16) for q, s in pairs]
    grown = [jnp.where(same, mmt(rows, spread), 0.0).astype(BF16) for rows in spreads]
    for (q, s), matrix in zip(pairs, grown):
        out = mm(matrix, stack[s]).astype(BF16)
        for k in range(KM):
            for h in range(GROUPS):
                w_ref[q, s, h * 16 : (h + 1) * 16, k * PAD : (k + 1) * PAD] = out[
                    k * 16 : (k + 1) * 16, h * PAD : (h + 1) * PAD
                ]


def observable_weights(first, lower, left_env, right_env, operators, after):
    return pl.pallas_call(
        lambda *refs: weight_kernel(first, *refs),
        out_shape=jax.ShapeDtypeStruct((2, HALF, PAD, SITE), BF16),
        in_specs=vmem(3) + anywhere(2),
        out_specs=vmem(1)[0],
        scratch_shapes=[
            pltpu.VMEM((HALF, WIDE, WIDE), BF16),
            pltpu.VMEM((HALF, WIDE, WIDE), BF16),
            pltpu.VMEM((HALF, PAD, SITE), BF16),
            pltpu.SemaphoreType.DMA((HALF,)),
        ],
        compiler_params=pltpu.CompilerParams(vmem_limit_bytes=16 << 20),
        cost_estimate=pl.CostEstimate(
            flops=3_000_000_000, bytes_accessed=2 << 20, transcendentals=0
        ),
        name="observable_weights",
    )(left_env, right_env, operators, after, lower)


def finish_kernel(entries, g_ref, *refs):
    *refs, low_ref, high_ref, out_ref, log_ref, obs_ref = refs
    us = refs
    row, col = lax.axis_index("row"), lax.axis_index("col")
    columns = g_ref.shape[0] // ROWS
    at_s = iota2((1, SEC), 1)
    at_qs, at_q = iota2((2, SEC), 1), iota2((2, SEC), 0)
    logs = jnp.zeros((1, SEC), F32)
    factors = []
    for i in range(ROWS):
        for k in range(2):
            scale = jnp.ones((columns, 1), F32)
            factor = jnp.zeros((columns, 1), F32)
            log = jnp.zeros((1, 1), F32)
            here = pl.ds(i * columns, columns)
            for r in range(ROWS):
                lane = 2 * ROWS * k + 2 * r
                squares = scale * scale * g_ref[here, lane + 1 : lane + 2]
                norm = jnp.sqrt(jnp.sum(squares, axis=0, keepdims=True) / entries + epsilon)
                scale = scale / norm
                factor = jnp.where(row == r, scale, factor)
                log = jnp.where(row == r, jnp.log(norm), log)
                scale = scale * g_ref[here, lane : lane + 1]
            at_col = iota2((columns, 1), 0) == col
            factors.append(jnp.sum(jnp.where(at_col, factor, 0.0), axis=0, keepdims=True))
            logs = jnp.where(at_s == 2 * i + k, log, logs)
    log_ref[...] = logs
    values = jnp.zeros((2, SEC), F32)
    for k in range(2):
        for x in range(ROWS):
            i = row ^ x
            s = 2 * i + k
            upper_half = i >= ROWS // 2
            at = s - jnp.where(upper_half, HALF, 0)
            factor = factors[k]
            for other in range(1, ROWS):
                factor = jnp.where(i == other, factors[2 * other + k], factor)
            u = us[x][k].astype(F32) * factor
            out_ref[s] = u.astype(BF16)
            for q in range(2):
                w = jnp.where(upper_half, high_ref[q, at].astype(F32), low_ref[q, at].astype(F32))
                value = total(u * w)
                values = jnp.where((at_q == q) & (at_qs == s), value, values)
    obs_ref[...] = values / math.sqrt(KM)


def finish(entries, gathered, weights, us):
    return pl.pallas_call(
        lambda *refs: finish_kernel(entries, *refs),
        out_shape=(
            jax.ShapeDtypeStruct((SEC, PAD, SITE), BF16),
            jax.ShapeDtypeStruct((1, SEC), F32),
            jax.ShapeDtypeStruct((2, SEC), F32),
        ),
        in_specs=vmem(3 + len(us)),
        out_specs=tuple(vmem(3)),
        compiler_params=pltpu.CompilerParams(vmem_limit_bytes=16 << 20),
        cost_estimate=pl.CostEstimate(flops=2_000_000, bytes_accessed=2 << 20, transcendentals=0),
        name="finish",
    )(gathered, *us, *weights)


def following(block):
    return passed_along(block, "col", -1)


def passed_along(block, axis, distance):
    devices = range(lax.axis_size(axis))
    route = [((i - distance) % len(devices), i) for i in devices]
    return lax.ppermute(block, axis, route)


def exchanged(block, x):
    return lax.ppermute(block, "row", [(i, i ^ x) for i in range(ROWS)])


NEAR_FIRST = (1, 3, 2)


def exchanged_all(blocks):
    got = {x: exchanged(blocks[x], x) for x in NEAR_FIRST}
    return [blocks[0]] + [got[x] for x in range(1, ROWS)]


def on_device(
    top_boundary, row_transfer, proj_in, proj_out, bottom_boundary, environments, operators, ranks
):
    columns = lax.axis_size("col")
    envs = environments[0, 0]
    lefts, transfers = proj_in[0, 0], row_transfer[0, 0]
    perm = bond_swap()
    lower = bottom_boundary[0, 0]
    *packed, q1, q2 = pack(0, ranks, lefts, transfers, ranks, proj_out[0, 0], envs)
    pts1 = exchanged_all(packed)
    next1, next2 = following(q1), following(q2)
    rights = mask_rights(ranks, ranks, next1)
    qs1 = exchanged_all(rights)
    low = observable_weights(0, lower, envs, next1, operators, rights[0])
    packed = pack(1, ranks, lefts, transfers, low, next2)
    ptqs2 = exchanged_all(packed)
    top = top_boundary[0]
    *us1, stats = chain(pts1, qs1, top, perm, None, (), packed[0], 8, "chain_first")
    high = observable_weights(HALF, lower, envs, next1, operators, stats)
    everyone = ROWS * columns
    *us, stats = chain(ptqs2, None, top, perm, stats, us1, high, everyone, "chain_second")
    us = exchanged_all(us)
    gathered = lax.all_to_all(stats, ("row", "col"), 0, 0, tiled=True)
    entries = float(columns * PAD * KM * PAD)
    sites, logs, values = finish(entries, gathered, (low, high), us)
    return sites[None, None], logs, values[:, None, None]


def solution(mesh):
    in_specs = (
        P("col", None, None, None),
        P("row", "col", None, None, None),
        P("row", "col", None, None, None),
        P("row", "col", None, None, None),
        P("row", "col", None, None, None),
        P("row", "col", None, None, None),
        P(),
        P("row", None),
    )
    out_specs = (P("row", "col", None, None, None), P("row", None), P(None, "row", "col", None))
    return jax.shard_map(
        on_device, mesh=mesh, in_specs=in_specs, out_specs=out_specs, check_vma=False
    )
```
